32 devices in a mesh: groups: 2 (over y), face: 4 (over z), band: 2 (over x), sub: 2 (over core).
Axes of the slice: x: 2, y: 2, z: 4, core: 2. Of those that a mesh axis runs over, the one named last changes fastest.
Arguments:
- grid_lat: bfloat16 [32768, 512], P(('groups', 'face', 'band', 'sub')), parts along dimension 0, may hold values from -6 to 6
- grid_route: int32 [32768, 1], P(('groups', 'face', 'band', 'sub')), parts along dimension 0, may hold values from 0 to 3; in each aligned block of 1024 rows (0 to 1023, 1024 to 2047, ...) at most 384 rows name the same one
- grid_slot: int32 [32768], P(('groups', 'face', 'band', 'sub')), parts along dimension 0, may hold values from 0 to 127
- mesh_lat: bfloat16 [4096, 512], P(('groups', 'face', 'band', 'sub')), parts along dimension 0, may hold values from -6 to 6
- mesh_nbr: int32 [4096, 6], P(('groups', 'face', 'band', 'sub')), parts along dimension 0, may hold values from 0 to 255
- enc_w1: bfloat16 [512, 512], P(('band', 'sub')), may hold values from -0.25 to 0.25
- enc_w2: bfloat16 [512, 512], P(('band', 'sub')), may hold values from -0.25 to 0.25
- grid_w1: bfloat16 [512, 512], P(('band', 'sub')), may hold values from -0.25 to 0.25
- grid_w2: bfloat16 [512, 512], P(('band', 'sub')), may hold values from -0.25 to 0.25
- node_w1: bfloat16 [1024, 512], P(('band', 'sub')), may hold values from -0.1875 to 0.1875
- node_w2: bfloat16 [512, 512], P(('band', 'sub')), may hold values from -0.25 to 0.25
- proc_w1: bfloat16 [1024, 512], P(('band', 'sub')), may hold values from -0.1875 to 0.1875
- proc_w2: bfloat16 [512, 512], P(('band', 'sub')), may hold values from -0.25 to 0.25
- upd_w1: bfloat16 [1024, 512], P(('band', 'sub')), may hold values from -0.1875 to 0.1875
- upd_w2: bfloat16 [512, 512], P(('band', 'sub')), may hold values from -0.25 to 0.25
Outputs:
- grid_out: bfloat16 [32768, 512], P(('groups', 'face', 'band', 'sub')), parts along dimension 0
- mesh_out: bfloat16 [4096, 512], P(('groups', 'face', 'band', 'sub')), parts along dimension 0
The draws below stay inside these ranges and needn't reach their ends.
There are 2 independent parts, one for each index of `groups`. The reference program is written for one: setup_inputs(seed, part) draws one part's arguments, and reference() takes and returns one part's arrays. A program takes and returns all parts, laid end to end along the dimension named above; an argument that names none is the same for every part. Nothing has to cross between parts.
Inputs may be any that keep to these rules, and one draw needn't show every extreme that they name: `grid_route`: among the rows of one device no face index is named more than 384 times, and some face index is named exactly 384 times.
All inputs are finite; a program needn't handle non-finite values.
Results may differ from the reference program's by a relative error of at most 0.009.
Values may be sent and summed in bfloat16 or wider, within the bound.
No kernel may reach another device: no remote copies, remote signals or barrier semaphores. Data moves between devices by JAX's collectives and lax.ppermute only.
A program may use at most 64 MiB of HBM per device.

```python
import math
import jax
import jax.numpy as jnp
import numpy as np
from jax import lax

D = 512
GRID_DEV = 1024
MESH_DEV = 128
NBRS = 6
HALO = 64
CAP = 384
GRID = 16384
MESH = 2048
N_FACE = 4
N_BAND = 2
N_SUB = 2


def with_ends(result, stream_key, low, top_value):
    extent = result.shape
    spot = [jax.random.randint(jax.random.fold_in(stream_key, axis), (), 0, extent[axis]) for axis in range(len(extent))]
    result = result.at[tuple(spot)].set(low)
    longest = extent.index(max(extent))
    spot[longest] = (spot[longest] + 1) % extent[longest]
    return result.at[tuple(spot)].set(top_value)


def levels(own_key, extent, cuts, smallest, high):
    gain = 1.0
    for axis_at, blocks in cuts:
        steps = jax.random.uniform(jax.random.fold_in(jax.random.fold_in(own_key, 6), axis_at), (blocks,), jnp.float32, smallest / len(cuts), high / len(cuts))
        gain = gain * jnp.repeat(jnp.exp(steps), extent[axis_at] // blocks).reshape((-1,) + (1,) * (len(extent) - 1 - axis_at))
    return gain


def assign_block(stream_key, own, number, rows, number_of, top, bound, skew):
    sequence = jax.random.permutation(stream_key, number_of)
    crowded, usual = load_shares(number_of, rows * top, bound, skew, True), load_shares(number_of, rows * top, bound, skew, False)
    places = jnp.arange(number_of)

    def named(sizes, rotation):
        used = int((sizes > 0).sum())
        fixed = max(1, used // 4)
        passed = fixed + (places - fixed + rotation * (used - fixed)) % max(1, number_of - fixed)
        return jnp.zeros((number_of,), jnp.int32).at[sequence[jnp.where(places < fixed, places, passed)]].set(jnp.asarray(sizes, jnp.int32))

    sizes = jnp.where(number % 4 == 0, named(crowded, number // 4), named(usual, number - number // 4 - 1))
    mixed = jax.random.permutation(jax.random.fold_in(own, 3), number_of)
    source_of, taker = mixed[0:number_of // 2 * 2:2], mixed[1:number_of // 2 * 2:2]
    slack = jnp.minimum(sizes[source_of] - 1, bound - sizes[taker]) // 2
    slack = jnp.where((source_of == sequence[0]) | (taker == sequence[0]) | (sizes[taker] == 0), 0, jnp.maximum(slack, 0))
    passed = jax.random.randint(jax.random.fold_in(own, 4), (number_of // 2,), 0, 1 << 20) % (slack + 1)
    sizes = sizes.at[source_of].add(-passed).at[taker].add(passed)
    items = jnp.searchsorted(jnp.cumsum(sizes), jnp.arange(rows * top), side="right").astype(jnp.int32)
    listing = items.reshape(top, rows).T
    listing = listing[jax.random.permutation(jax.random.fold_in(own, 1), rows)]
    rotation = jax.random.randint(jax.random.fold_in(own, 2), (rows, 1), 0, top)
    return jnp.take_along_axis(listing, (jnp.arange(top)[None, :] + rotation) % top, axis=1)


def load_shares(amount, total, bound, lean, full):
    portions = [(1 << 20) // math.isqrt(grade ** lean) + 1 for grade in range(1, amount + 1)]
    largest = bound if full else min(bound, max(-(-total // amount), total * portions[0] // sum(portions)))
    least = 1 if total - largest >= amount - 1 else 0
    counts, spare = [largest] + [least] * (amount - 1), total - largest - least * (amount - 1)
    while spare > 0:
        free = [i for i in range(1, amount) if counts[i] < largest] or [i for i in range(1, amount) if counts[i] < bound]
        pool, remaining = sum([portions[i] for i in free]), spare
        for i in free:
            addition = min(bound - counts[i], max(1, remaining * portions[i] // pool), spare)
            counts[i] = counts[i] + addition
            spare = spare - addition
    return np.array(counts)


def bell_draw(own_key, dims, width, reach, cuts=(), kind=jnp.bfloat16):
    values = jax.random.normal(own_key, dims, jnp.float32) * width
    if len(cuts) > 0:
        values = levels(own_key, dims, cuts, -0.22, 0.18) * values
    return jnp.clip(values, min=-reach, max=reach).astype(kind)


def setup_inputs(seed: int = 0, part: int = 0) -> dict:
    seeds = jax.random.split(jax.random.key(seed), 16)
    own_keys = jax.random.split(jax.random.fold_in(seeds[15], part), 16)
    grid_lat = bell_draw(own_keys[0], (GRID, D), 1.0, 6.0, ((0, 16),))
    grid_route_keys = jax.random.split(jax.random.fold_in(own_keys[1], 1), GRID // GRID_DEV)
    grid_route_turns = jax.random.permutation(jax.random.fold_in(own_keys[1], 3), GRID // GRID_DEV)
    grid_route = jax.vmap(lambda own, number: assign_block(jax.random.fold_in(own_keys[1], 2), own, number, GRID_DEV, N_FACE, 1, CAP, 2))(grid_route_keys, grid_route_turns).reshape((GRID, 1))
    grid_slot = with_ends(jax.random.randint(own_keys[2], (GRID,), 0, MESH_DEV), jax.random.fold_in(own_keys[2], 1), 0, MESH_DEV - 1).astype(jnp.int32)
    mesh_lat = bell_draw(own_keys[3], (MESH, D), 1.0, 6.0, ((0, 16),))
    mesh_nbr = with_ends(jax.random.randint(own_keys[4], (MESH, NBRS), 0, MESH_DEV + 2 * HALO), jax.random.fold_in(own_keys[4], 1), 0, (MESH_DEV + 2 * HALO) - 1).astype(jnp.int32)
    enc_w1 = bell_draw(seeds[5], (D, D), D ** -0.5, 0.25, ((0, 4),))
    enc_w2 = bell_draw(seeds[6], (D, D), D ** -0.5, 0.25, ((0, 4),))
    grid_w1 = bell_draw(seeds[7], (D, D), D ** -0.5, 0.25, ((0, 4),))
    grid_w2 = bell_draw(seeds[8], (D, D), D ** -0.5, 0.25, ((0, 4),))
    node_w1 = bell_draw(seeds[9], (2 * D, D), (2 * D) ** -0.5, 0.1875, ((0, 4),))
    node_w2 = bell_draw(seeds[10], (D, D), D ** -0.5, 0.25, ((0, 4),))
    proc_w1 = bell_draw(seeds[11], (2 * D, D), (2 * D) ** -0.5, 0.1875, ((0, 4),))
    proc_w2 = bell_draw(seeds[12], (D, D), D ** -0.5, 0.25, ((0, 4),))
    upd_w1 = bell_draw(seeds[13], (2 * D, D), (2 * D) ** -0.5, 0.1875, ((0, 4),))
    upd_w2 = bell_draw(seeds[14], (D, D), D ** -0.5, 0.25, ((0, 4),))
    return {"grid_lat": grid_lat, "grid_route": grid_route, "grid_slot": grid_slot, "mesh_lat": mesh_lat, "mesh_nbr": mesh_nbr, "enc_w1": enc_w1, "enc_w2": enc_w2, "grid_w1": grid_w1, "grid_w2": grid_w2, "node_w1": node_w1, "node_w2": node_w2, "proc_w1": proc_w1, "proc_w2": proc_w2, "upd_w1": upd_w1, "upd_w2": upd_w2}


def layer_norm(values):
    average = lax.optimization_barrier(jnp.mean(values, axis=-1, keepdims=True))
    centred = values - average
    spread = lax.optimization_barrier(jnp.mean(centred * centred, axis=-1, keepdims=True))
    return centred * lax.rsqrt(spread + 1e-05)

def perceptron(inputs, weight_in, weight_out):
    hidden = jax.nn.silu(jnp.dot(inputs, weight_in, preferred_element_type=jnp.float32)).astype(jnp.bfloat16)
    return layer_norm(jnp.dot(hidden, weight_out, preferred_element_type=jnp.float32))

def reference(grid_lat, grid_route, grid_slot, mesh_lat, mesh_nbr, enc_w1, enc_w2, grid_w1, grid_w2, node_w1, node_w2, proc_w1, proc_w2, upd_w1, upd_w2):
    devices = N_FACE * N_BAND * N_SUB
    lane_count = N_BAND * N_SUB
    grid_blocks = grid_lat.reshape(devices, GRID_DEV, D)

    def encode_block(rows_block):
        messages = perceptron(rows_block, enc_w1, enc_w2).astype(jnp.bfloat16)
        updated = (rows_block.astype(jnp.float32) + perceptron(rows_block, grid_w1, grid_w2)).astype(jnp.bfloat16)
        return (messages, updated)
    messages, grid_out = lax.map(encode_block, grid_blocks)
    lane_index = jnp.arange(devices, dtype=jnp.int32)[:, None] % lane_count
    targets = (grid_route.reshape(devices, GRID_DEV) * lane_count + lane_index) * MESH_DEV + grid_slot.reshape(devices, GRID_DEV)
    collected = jax.ops.segment_sum(messages.reshape(-1, D).astype(jnp.float32), targets.reshape(-1).astype(jnp.int32), num_segments=devices * MESH_DEV)
    mesh_in = jnp.concatenate([mesh_lat, collected.astype(jnp.bfloat16)], axis=1)
    mesh_mid = (mesh_lat.astype(jnp.float32) + perceptron(mesh_in, node_w1, node_w2)).astype(jnp.bfloat16)
    mesh_grid = mesh_mid.reshape(N_FACE, lane_count, MESH_DEV, D)
    before = jnp.roll(mesh_grid, 1, axis=0)[:, :, MESH_DEV - HALO:, :]
    after = jnp.roll(mesh_grid, -1, axis=0)[:, :, :HALO, :]
    extended = jnp.concatenate([before, mesh_grid, after], axis=2).reshape(devices, MESH_DEV + 2 * HALO, D)
    neighbours = mesh_nbr.reshape(devices, MESH_DEV * NBRS)

    def process_block(operands):
        rows_ext, indices, own_rows = operands
        senders = rows_ext[indices]
        receivers = jnp.repeat(own_rows, NBRS, axis=0)
        edges = perceptron(jnp.concatenate([senders, receivers], axis=1), proc_w1, proc_w2)
        edge_sum = lax.optimization_barrier(jnp.sum(edges.reshape(MESH_DEV, NBRS, D), axis=1)).astype(jnp.bfloat16)
        joined = jnp.concatenate([own_rows, edge_sum], axis=1)
        return (own_rows.astype(jnp.float32) + perceptron(joined, upd_w1, upd_w2)).astype(jnp.bfloat16)
    mesh_out = lax.map(process_block, (extended, neighbours, mesh_mid.reshape(devices, MESH_DEV, D)))
    return (grid_out.reshape(-1, D), mesh_out.reshape(-1, D))
```

```python
import functools

import jax
import jax.numpy as jnp
from jax import lax
from jax.experimental import pallas as pl
from jax.experimental.pallas import tpu as pltpu
from jax.sharding import PartitionSpec as P

MIB = 1 << 20
ANY = pl.BlockSpec(memory_space=pl.ANY)
VMEM = pl.BlockSpec(memory_space=pltpu.VMEM)


def after(value, *earlier):
    return lax.optimization_barrier((value, *earlier))[0]


def shift(value, axis, step):
    count = lax.axis_size(axis)
    return lax.ppermute(value, axis, [(i, (i + step) % count) for i in range(count)])


def spread(pack, *earlier):
    bands, subs = lax.axis_size("band"), lax.axis_size("sub")
    first = after(pack, *earlier) if earlier else pack
    rows = [pack] + [shift(first, "band", step) for step in range(1, bands)]
    pieces = []
    for row in rows:
        pieces.append(row)
        pieces.extend(shift(row, "sub", step) for step in range(1, subs))
    return pieces, rows[-1]


def load_copies(pieces, parts, sems):
    bands, subs = lax.axis_size("band"), lax.axis_size("sub")
    band, sub = lax.axis_index("band"), lax.axis_index("sub")
    copies = []
    for index, piece in enumerate(pieces):
        owner = lax.rem(band + bands - index // subs, bands) * subs + lax.rem(
            sub + subs - index % subs, subs
        )
        start = 0
        for part, (rows, whole) in enumerate(parts):
            copies.append(
                pltpu.make_async_copy(
                    piece.at[pl.ds(start, rows)],
                    whole.at[pl.ds(pl.multiple_of(owner * rows, rows), rows)],
                    sems.at[part, index],
                )
            )
            start += rows
    return copies


def silu(values):
    half = 0.5 * values
    return half + half * jnp.tanh(half)


def layer_norm(values):
    average = jnp.mean(values, axis=-1, keepdims=True)
    centred = values - average
    spread_of = jnp.mean(centred * centred, axis=-1, keepdims=True)
    return centred * lax.rsqrt(spread_of + 1e-05)


def dot(a, b):
    return jnp.dot(a, b, preferred_element_type=jnp.float32)


def encode_kernel(count, faces, mesh_rows, target_ref, lat_ref, *refs):
    in_pieces, hid_pieces = refs[:count], refs[count : 2 * count]
    outs = refs[2 * count : 2 * count + faces]
    w_in, w_hid, messages, sems_in, sems_hid = refs[2 * count + faces :]
    rows = w_in.shape[0] // count
    first = load_copies(in_pieces, [(rows, w_in)], sems_in)
    second = load_copies(hid_pieces, [(rows, w_hid)], sems_hid)
    for copy in first + second:
        copy.start()
    for copy in first + second:
        copy.wait()
    block = 256
    for start in range(0, lat_ref.shape[0], block):
        here = pl.ds(start, block)
        hidden = silu(dot(lat_ref[here], w_in[...])).astype(jnp.bfloat16)
        messages[here] = layer_norm(dot(hidden, w_hid[...])).astype(jnp.bfloat16)
    group = min(faces, 4)
    for at in range(0, faces, group):
        slots = lax.broadcasted_iota(jnp.int32, (group * mesh_rows, lat_ref.shape[0]), 0)
        chosen = jnp.where(slots + at * mesh_rows == target_ref[...], 1.0, 0.0)
        chosen = chosen.astype(jnp.bfloat16)
        sums = dot(chosen, messages[...])
        for face in range(group):
            out = outs[at + face]
            out[...] = sums[face * mesh_rows : (face + 1) * mesh_rows].astype(out.dtype)


def grid_kernel(count, lat_ref, *refs):
    pieces = refs[:count]
    out_ref, w_in, w_hid, sems = refs[count:]
    rows = w_in.shape[0] // count
    copies = load_copies(pieces, [(rows, w_in), (rows, w_hid)], sems)
    for copy in copies:
        copy.start()
    for copy in copies:
        copy.wait()
    block = 256
    for start in range(0, lat_ref.shape[0], block):
        here = pl.ds(start, block)
        lat = lat_ref[here]
        hidden = silu(dot(lat, w_in[...])).astype(jnp.bfloat16)
        out = lat.astype(jnp.float32) + layer_norm(dot(hidden, w_hid[...]))
        out_ref[here] = out.astype(jnp.bfloat16)


def node_kernel(count, faces, lat_ref, *refs):
    sums, pieces = refs[:faces], refs[faces : faces + count]
    head_ref, tail_ref, w_in, w_hid, sems = refs[faces + count :]
    width = lat_ref.shape[1]
    copies = load_copies(
        pieces, [(w_in.shape[0] // count, w_in), (w_hid.shape[0] // count, w_hid)], sems
    )
    for copy in copies:
        copy.start()
    collected = sums[0][...]
    for one in sums[1:]:
        collected = collected + one[...].astype(jnp.float32)
    for copy in copies:
        copy.wait()
    lat = lat_ref[...]
    hidden = dot(lat, w_in[:width]) + dot(collected.astype(jnp.bfloat16), w_in[width:])
    hidden = silu(hidden).astype(jnp.bfloat16)
    mid = lat.astype(jnp.float32) + layer_norm(dot(hidden, w_hid[...]))
    mid = mid.astype(jnp.bfloat16)
    half = mid.shape[0] // 2
    head_ref[...] = mid[:half]
    tail_ref[...] = mid[half:]


def edge_kernel(count, nbr_ref, before_ref, head_ref, tail_ref, after_ref, *refs):
    proc, upd = refs[:count], refs[count : 2 * count]
    out_ref, p_in, p_hid, u_in, u_hid, sems_p, sems_u = refs[2 * count :]
    copies_p = load_copies(
        proc, [(p_in.shape[0] // count, p_in), (p_hid.shape[0] // count, p_hid)], sems_p
    )
    copies_u = load_copies(
        upd, [(u_in.shape[0] // count, u_in), (u_hid.shape[0] // count, u_hid)], sems_u
    )
    for copy in copies_p + copies_u:
        copy.start()
    rows, fanin = nbr_ref.shape
    width = head_ref.shape[1]
    mid = jnp.concatenate([head_ref[...], tail_ref[...]], axis=0)
    extended = jnp.concatenate([before_ref[...], mid, after_ref[...]], axis=0)
    spots = lax.broadcasted_iota(jnp.int32, (rows, extended.shape[0]), 1)
    nbr = nbr_ref[...]
    for copy in copies_p:
        copy.wait()
    receivers = dot(mid, p_in[width:])
    total = None
    group = 2 if fanin % 2 == 0 else 1
    for at in range(0, fanin, group):
        chosen = jnp.concatenate(
            [
                jnp.where(spots == nbr[:, k : k + 1], 1.0, 0.0).astype(jnp.bfloat16)
                for k in range(at, at + group)
            ],
            axis=0,
        )
        senders = dot(chosen, extended).astype(jnp.bfloat16)
        hidden = dot(senders, p_in[:width])
        hidden = (hidden.reshape(group, rows, width) + receivers[None]).reshape(group * rows, width)
        edges = layer_norm(dot(silu(hidden).astype(jnp.bfloat16), p_hid[...]))
        for k in range(group):
            one = edges[k * rows : (k + 1) * rows]
            total = one if total is None else total + one
    for copy in copies_u:
        copy.wait()
    hidden = dot(mid, u_in[:width]) + dot(total.astype(jnp.bfloat16), u_in[width:])
    hidden = silu(hidden).astype(jnp.bfloat16)
    out = mid.astype(jnp.float32) + layer_norm(dot(hidden, u_hid[...]))
    out_ref[...] = out.astype(jnp.bfloat16)


def shards(
    grid_lat,
    grid_route,
    grid_slot,
    mesh_lat,
    mesh_nbr,
    enc_w1,
    enc_w2,
    grid_w1,
    grid_w2,
    node_w1,
    node_w2,
    proc_w1,
    proc_w2,
    upd_w1,
    upd_w2,
):
    grid_rows, width = grid_lat.shape
    mesh_rows = mesh_lat.shape[0]
    faces = lax.axis_size("face")
    count = lax.axis_size("band") * lax.axis_size("sub")
    f32, bf16 = jnp.float32, jnp.bfloat16

    def matrix(weight):
        return pltpu.VMEM((weight.shape[0] * count, weight.shape[1]), bf16)

    def sems(parts):
        return pltpu.SemaphoreType.DMA((parts, count))

    def cost(rows, depth):
        return pl.CostEstimate(
            flops=2 * rows * depth * width,
            bytes_accessed=2 * (rows + depth) * width,
            transcendentals=rows * width,
        )

    enc_in, enc_in_last = spread(enc_w1)
    enc_hid, enc_hid_last = spread(enc_w2)
    node, node_last = spread(
        jnp.concatenate([node_w1, node_w2], axis=0), enc_in_last, enc_hid_last
    )
    grid, grid_last = spread(jnp.concatenate([grid_w1, grid_w2], axis=0), node_last)
    proc, proc_last = spread(jnp.concatenate([proc_w1, proc_w2], axis=0), grid_last)
    upd, _ = spread(jnp.concatenate([upd_w1, upd_w2], axis=0), proc_last)

    me = lax.axis_index("face")
    distance = lax.rem(grid_route[:, 0] - me + faces, faces)
    targets = (distance * mesh_rows + grid_slot).reshape(1, grid_rows)

    block = (mesh_rows, width)
    sums = pl.pallas_call(
        functools.partial(encode_kernel, count, faces, mesh_rows),
        out_shape=[
            jax.ShapeDtypeStruct(block, bf16 if step else f32) for step in range(faces)
        ],
        in_specs=[VMEM, VMEM] + [ANY] * (2 * count),
        out_specs=[VMEM] * faces,
        scratch_shapes=[
            matrix(enc_w1),
            matrix(enc_w2),
            pltpu.VMEM((grid_rows, width), bf16),
            sems(1),
            sems(1),
        ],
        compiler_params=pltpu.CompilerParams(vmem_limit_bytes=32 * MIB),
        cost_estimate=cost(grid_rows, 3 * width),
        name="encode",
    )(targets, grid_lat, *enc_in, *enc_hid)
    arrived = [sums[0]] + [shift(sums[step], "face", step) for step in range(1, faces)]

    grid_out = pl.pallas_call(
        functools.partial(grid_kernel, count),
        out_shape=jax.ShapeDtypeStruct(grid_lat.shape, bf16),
        in_specs=[VMEM] + [ANY] * count,
        out_specs=VMEM,
        scratch_shapes=[matrix(grid_w1), matrix(grid_w2), sems(2)],
        compiler_params=pltpu.CompilerParams(vmem_limit_bytes=32 * MIB),
        cost_estimate=cost(grid_rows, 2 * width),
        name="grid_update",
    )(grid_lat, *grid)

    half = (mesh_rows // 2, width)
    head, tail = pl.pallas_call(
        functools.partial(node_kernel, count, faces),
        out_shape=[jax.ShapeDtypeStruct(half, bf16)] * 2,
        in_specs=[VMEM] * (1 + faces) + [ANY] * count,
        out_specs=[VMEM] * 2,
        scratch_shapes=[matrix(node_w1), matrix(node_w2), sems(2)],
        compiler_params=pltpu.CompilerParams(vmem_limit_bytes=32 * MIB),
        cost_estimate=cost(mesh_rows, 3 * width),
        name="node_update",
    )(mesh_lat, *arrived, *node)

    before = shift(tail, "face", 1)
    behind = shift(head, "face", faces - 1)
    mesh_out = pl.pallas_call(
        functools.partial(edge_kernel, count),
        out_shape=jax.ShapeDtypeStruct(mesh_lat.shape, bf16),
        in_specs=[VMEM] * 5 + [ANY] * (2 * count),
        out_specs=VMEM,
        scratch_shapes=[
            matrix(proc_w1),
            matrix(proc_w2),
            matrix(upd_w1),
            matrix(upd_w2),
            sems(2),
            sems(2),
        ],
        compiler_params=pltpu.CompilerParams(vmem_limit_bytes=32 * MIB),
        cost_estimate=cost(mesh_rows * mesh_nbr.shape[1], 3 * width),
        name="edge_update",
    )(mesh_nbr, before, head, tail, behind, *proc, *upd)
    return (grid_out, mesh_out)


def solution(mesh):
    rows = ("groups", "face", "band", "sub")
    placed = (
        P(rows, None),
        P(rows, None),
        P(rows),
        P(rows, None),
        P(rows, None),
    ) + (P(("band", "sub"), None),) * 10
    return jax.shard_map(
        shards,
        mesh=mesh,
        in_specs=placed,
        out_specs=(P(rows, None), P(rows, None)),
        check_vma=False,
    )
```

```python
import functools

import jax
import jax.numpy as jnp
from jax import lax
from jax.experimental import pallas as pl
from jax.experimental.pallas import tpu as pltpu
from jax.sharding import PartitionSpec as P

MIB = 1 << 20
ANY = pl.BlockSpec(memory_space=pl.ANY)
VMEM = pl.BlockSpec(memory_space=pltpu.VMEM)


def after(value, *earlier):
    return lax.optimization_barrier((value, *earlier))[0]


def shift(value, axis, step):
    count = lax.axis_size(axis)
    return lax.ppermute(value, axis, [(i, (i + step) % count) for i in range(count)])


def spread(pack):
    bands, subs = lax.axis_size("band"), lax.axis_size("sub")
    rows = [pack] + [shift(pack, "band", step) for step in range(1, bands)]
    pieces = []
    for row in rows:
        pieces.append(row)
        pieces.extend(shift(row, "sub", step) for step in range(1, subs))
    return pieces, rows[1:]


def own_spread(pack):
    return [pack] + [shift(pack, "sub", step) for step in range(1, lax.axis_size("sub"))]


def relay(parts, *earlier):
    pieces = []
    for part in parts:
        first = after(part, *earlier) if earlier else part
        for far in range(lax.axis_size("groups")):
            held = shift(first, "groups", far) if far else part
            pieces.extend([held] + [shift(held, "sub", near) for near in range(1, lax.axis_size("sub"))])
    return pieces


def owner_of(band_step, sub_step):
    bands, subs = lax.axis_size("band"), lax.axis_size("sub")
    return lax.rem(lax.axis_index("band") + bands - band_step, bands) * subs + lax.rem(
        lax.axis_index("sub") + subs - sub_step, subs
    )


def load_copies(pieces, rows, whole, sems):
    subs = lax.axis_size("sub")
    copies = []
    for index, piece in enumerate(pieces):
        owner = owner_of(index // subs, index % subs)
        there = whole.at[pl.ds(pl.multiple_of(owner * rows, rows), rows)]
        copies.append(pltpu.make_async_copy(piece, there, sems.at[index]))
    return copies


def pack_copies(pieces, sizes, wanted, sems):
    subs, groups = lax.axis_size("sub"), lax.axis_size("groups")
    block = sum(sizes) // groups
    group = lax.axis_index("groups")
    copies = []
    slot = 0
    for index, piece in enumerate(pieces):
        if index < subs:
            owner = owner_of(0, index)
            held = [(part, part * block) for part in range(groups)]
        else:
            band_step, rest = divmod(index - subs, groups * subs)
            far, near = divmod(rest, subs)
            owner = owner_of(band_step + 1, near)
            held = [(lax.rem(group + groups - far, groups), 0)]
        for part, base in held:
            for at, whole in wanted.items():
                rows = sizes[at] // groups
                start = base + sum(sizes[:at]) // groups
                into = pl.multiple_of(owner * sizes[at] + part * rows, rows)
                copies.append(
                    pltpu.make_async_copy(
                        piece.at[pl.ds(start, rows)], whole.at[pl.ds(into, rows)], sems.at[slot]
                    )
                )
                slot += 1
    return copies


def pack_kernel(sets, *refs):
    count = sum(sets)
    sources, outs, sems = refs[:count], refs[count:-1], refs[-1]
    groups = lax.axis_size("groups")
    group = lax.axis_index("groups")
    copies = []
    first = 0
    for at, amount in enumerate(sets):
        pack, mine = outs[2 * at], outs[2 * at + 1]
        start = 0
        for part in range(groups + 1):
            into, chosen, base = (pack, part, start) if part < groups else (mine, group, 0)
            for source in sources[first : first + amount]:
                rows = source.shape[0] // groups
                begin = chosen * rows if part < groups else pl.multiple_of(chosen * rows, rows)
                copies.append(
                    pltpu.make_async_copy(
                        source.at[pl.ds(begin, rows)], into.at[pl.ds(base, rows)], sems.at[len(copies)]
                    )
                )
                base += rows
            start = base
        first += amount
    for copy in copies:
        copy.start()
    for copy in copies:
        copy.wait()


def silu(values):
    half = 0.5 * values
    return half + half * jnp.tanh(half)


def layer_norm(values):
    average = jnp.mean(values, axis=-1, keepdims=True)
    centred = values - average
    spread_of = jnp.mean(centred * centred, axis=-1, keepdims=True)
    return centred * lax.rsqrt(spread_of + 1e-05)


def dot(a, b):
    return jnp.dot(a, b, preferred_element_type=jnp.float32)


def encode_kernel(count, faces, mesh_rows, target_ref, lat_ref, *refs):
    in_pieces, hid_pieces = refs[:count], refs[count : 2 * count]
    outs = refs[2 * count : 2 * count + faces]
    w_in, w_hid, messages, sems_in, sems_hid = refs[2 * count + faces :]
    rows = w_in.shape[0] // count
    first = load_copies(in_pieces, rows, w_in, sems_in)
    second = load_copies(hid_pieces, rows, w_hid, sems_hid)
    for copy in first + second:
        copy.start()
    for copy in first + second:
        copy.wait()
    block = 256
    for start in range(0, lat_ref.shape[0], block):
        here = pl.ds(start, block)
        hidden = silu(dot(lat_ref[here], w_in[...])).astype(jnp.bfloat16)
        messages[here] = layer_norm(dot(hidden, w_hid[...])).astype(jnp.bfloat16)
    group = min(faces, 4)
    for at in range(0, faces, group):
        slots = lax.broadcasted_iota(jnp.int32, (group * mesh_rows, lat_ref.shape[0]), 0)
        chosen = jnp.where(slots + at * mesh_rows == target_ref[...], 1.0, 0.0)
        chosen = chosen.astype(jnp.bfloat16)
        sums = dot(chosen, messages[...])
        for face in range(group):
            out = outs[at + face]
            out[...] = sums[face * mesh_rows : (face + 1) * mesh_rows].astype(out.dtype)


def grid_kernel(sizes, lat_ref, *refs):
    pieces, (out_ref, w_in, w_hid, sems) = refs[:-4], refs[-4:]
    copies = pack_copies(pieces, sizes, {2: w_in, 3: w_hid}, sems)
    for copy in copies:
        copy.start()
    for copy in copies:
        copy.wait()
    block = 256
    for start in range(0, lat_ref.shape[0], block):
        here = pl.ds(start, block)
        lat = lat_ref[here]
        hidden = silu(dot(lat, w_in[...])).astype(jnp.bfloat16)
        out = lat.astype(jnp.float32) + layer_norm(dot(hidden, w_hid[...]))
        out_ref[here] = out.astype(jnp.bfloat16)


def node_kernel(sizes, faces, lat_ref, *refs):
    sums, pieces = refs[:faces], refs[faces:-5]
    head_ref, tail_ref, w_in, w_hid, sems = refs[-5:]
    width = lat_ref.shape[1]
    copies = pack_copies(pieces, sizes, {0: w_in, 1: w_hid}, sems)
    for copy in copies:
        copy.start()
    collected = sums[0][...]
    for one in sums[1:]:
        collected = collected + one[...].astype(jnp.float32)
    for copy in copies:
        copy.wait()
    lat = lat_ref[...]
    hidden = dot(lat, w_in[:width]) + dot(collected.astype(jnp.bfloat16), w_in[width:])
    hidden = silu(hidden).astype(jnp.bfloat16)
    mid = lat.astype(jnp.float32) + layer_norm(dot(hidden, w_hid[...]))
    mid = mid.astype(jnp.bfloat16)
    half = mid.shape[0] // 2
    head_ref[...] = mid[:half]
    tail_ref[...] = mid[half:]


def edge_kernel(sizes, nbr_ref, before_ref, head_ref, tail_ref, after_ref, *refs):
    pieces, (out_ref, p_in, p_hid, u_in, u_hid, sems_p, sems_u) = refs[:-7], refs[-7:]
    copies_p = pack_copies(pieces, sizes, {0: p_in, 1: p_hid}, sems_p)
    copies_u = pack_copies(pieces, sizes, {2: u_in, 3: u_hid}, sems_u)
    for copy in copies_p + copies_u:
        copy.start()
    rows, fanin = nbr_ref.shape
    width = head_ref.shape[1]
    mid = jnp.concatenate([head_ref[...], tail_ref[...]], axis=0)
    extended = jnp.concatenate([before_ref[...], mid, after_ref[...]], axis=0)
    spots = lax.broadcasted_iota(jnp.int32, (rows, extended.shape[0]), 1)
    nbr = nbr_ref[...]
    for copy in copies_p:
        copy.wait()
    receivers = dot(mid, p_in[width:])
    total = None
    group = 2 if fanin % 2 == 0 else 1
    for at in range(0, fanin, group):
        chosen = jnp.concatenate(
            [
                jnp.where(spots == nbr[:, k : k + 1], 1.0, 0.0).astype(jnp.bfloat16)
                for k in range(at, at + group)
            ],
            axis=0,
        )
        senders = dot(chosen, extended).astype(jnp.bfloat16)
        hidden = dot(senders, p_in[:width])
        hidden = (hidden.reshape(group, rows, width) + receivers[None]).reshape(group * rows, width)
        edges = layer_norm(dot(silu(hidden).astype(jnp.bfloat16), p_hid[...]))
        for k in range(group):
            one = edges[k * rows : (k + 1) * rows]
            total = one if total is None else total + one
    for copy in copies_u:
        copy.wait()
    hidden = dot(mid, u_in[:width]) + dot(total.astype(jnp.bfloat16), u_in[width:])
    hidden = silu(hidden).astype(jnp.bfloat16)
    out = mid.astype(jnp.float32) + layer_norm(dot(hidden, u_hid[...]))
    out_ref[...] = out.astype(jnp.bfloat16)


def shards(
    grid_lat,
    grid_route,
    grid_slot,
    mesh_lat,
    mesh_nbr,
    enc_w1,
    enc_w2,
    grid_w1,
    grid_w2,
    node_w1,
    node_w2,
    proc_w1,
    proc_w2,
    upd_w1,
    upd_w2,
):
    grid_rows, width = grid_lat.shape
    mesh_rows = mesh_lat.shape[0]
    faces = lax.axis_size("face")
    count = lax.axis_size("band") * lax.axis_size("sub")
    f32, bf16 = jnp.float32, jnp.bfloat16

    def matrix(weight):
        return pltpu.VMEM((weight.shape[0] * count, weight.shape[1]), bf16)

    groups, subs, bands = lax.axis_size("groups"), lax.axis_size("sub"), lax.axis_size("band")
    copies = groups * count

    def sems(parts):
        return pltpu.SemaphoreType.DMA((parts,))

    def cost(rows, depth):
        return pl.CostEstimate(
            flops=2 * rows * depth * width,
            bytes_accessed=2 * (rows + depth) * width,
            transcendentals=rows * width,
        )

    sets = ((node_w1, node_w2, grid_w1, grid_w2), (proc_w1, proc_w2, upd_w1, upd_w2))
    sizes = [[weight.shape[0] for weight in one] for one in sets]
    early, early_mine, late, late_mine = pl.pallas_call(
        functools.partial(pack_kernel, [len(one) for one in sets]),
        out_shape=[
            jax.ShapeDtypeStruct((sum(one) // part, width), bf16)
            for one in sizes
            for part in (1, groups)
        ],
        in_specs=[ANY] * 8,
        out_specs=[ANY] * 4,
        scratch_shapes=[sems(8 * (groups + 1))],
        name="pack",
    )(*sets[0], *sets[1])

    enc_in, enc_in_far = spread(enc_w1)
    enc_hid, enc_hid_far = spread(enc_w2)
    early_near, late_near = own_spread(early), own_spread(late)
    early_sent = after(early_mine, *enc_in_far, *enc_hid_far)
    early_far = [shift(early_sent, "band", step) for step in range(1, bands)]

    me = lax.axis_index("face")
    distance = lax.rem(grid_route[:, 0] - me + faces, faces)
    targets = (distance * mesh_rows + grid_slot).reshape(1, grid_rows)

    block = (mesh_rows, width)
    sums = pl.pallas_call(
        functools.partial(encode_kernel, count, faces, mesh_rows),
        out_shape=[
            jax.ShapeDtypeStruct(block, bf16 if step else f32) for step in range(faces)
        ],
        in_specs=[VMEM, VMEM] + [ANY] * (2 * count),
        out_specs=[VMEM] * faces,
        scratch_shapes=[
            matrix(enc_w1),
            matrix(enc_w2),
            pltpu.VMEM((grid_rows, width), bf16),
            sems(count),
            sems(count),
        ],
        compiler_params=pltpu.CompilerParams(vmem_limit_bytes=32 * MIB),
        cost_estimate=cost(grid_rows, 3 * width),
        name="encode",
    )(targets, grid_lat, *enc_in, *enc_hid)
    early_all = early_near + relay(early_far, sums[0])
    late_sent = after(late_mine, sums[0], *early_far)
    late_far = [shift(late_sent, "band", step) for step in range(1, bands)]
    arrived = [sums[0]] + [shift(sums[step], "face", step) for step in range(1, faces)]

    grid_out = pl.pallas_call(
        functools.partial(grid_kernel, sizes[0]),
        out_shape=jax.ShapeDtypeStruct(grid_lat.shape, bf16),
        in_specs=[VMEM] + [ANY] * len(early_all),
        out_specs=VMEM,
        scratch_shapes=[matrix(grid_w1), matrix(grid_w2), sems(2 * copies)],
        compiler_params=pltpu.CompilerParams(vmem_limit_bytes=32 * MIB),
        cost_estimate=cost(grid_rows, 2 * width),
        name="grid_update",
    )(after(grid_lat, *late_far), *early_all)

    half = (mesh_rows // 2, width)
    head, tail = pl.pallas_call(
        functools.partial(node_kernel, sizes[0], faces),
        out_shape=[jax.ShapeDtypeStruct(half, bf16)] * 2,
        in_specs=[VMEM] * (1 + faces) + [ANY] * len(early_all),
        out_specs=[VMEM] * 2,
        scratch_shapes=[matrix(node_w1), matrix(node_w2), sems(2 * copies)],
        compiler_params=pltpu.CompilerParams(vmem_limit_bytes=32 * MIB),
        cost_estimate=cost(mesh_rows, 3 * width),
        name="node_update",
    )(mesh_lat, *arrived, *early_all)

    before = shift(tail, "face", 1)
    behind = shift(head, "face", faces - 1)
    late_all = late_near + relay(late_far)
    mesh_out = pl.pallas_call(
        functools.partial(edge_kernel, sizes[1]),
        out_shape=jax.ShapeDtypeStruct(mesh_lat.shape, bf16),
        in_specs=[VMEM] * 5 + [ANY] * len(late_all),
        out_specs=VMEM,
        scratch_shapes=[
            matrix(proc_w1),
            matrix(proc_w2),
            matrix(upd_w1),
            matrix(upd_w2),
            sems(2 * copies),
            sems(2 * copies),
        ],
        compiler_params=pltpu.CompilerParams(vmem_limit_bytes=32 * MIB),
        cost_estimate=cost(mesh_rows * mesh_nbr.shape[1], 3 * width),
        name="edge_update",
    )(mesh_nbr, before, head, tail, behind, *late_all)
    return (grid_out, mesh_out)


def solution(mesh):
    rows = ("groups", "face", "band", "sub")
    placed = (
        P(rows, None),
        P(rows, None),
        P(rows),
        P(rows, None),
        P(rows, None),
    ) + (P(("band", "sub"), None),) * 10
    return jax.shard_map(
        shards,
        mesh=mesh,
        in_specs=placed,
        out_specs=(P(rows, None), P(rows, None)),
        check_vma=False,
    )
```

```python
import functools

import jax
import jax.numpy as jnp
from jax import lax
from jax.experimental import pallas as pl
from jax.experimental.pallas import tpu as pltpu
from jax.sharding import PartitionSpec as P

MIB = 1 << 20
ANY = pl.BlockSpec(memory_space=pl.ANY)
VMEM = pl.BlockSpec(memory_space=pltpu.VMEM)


def after(value, *earlier):
    return lax.optimization_barrier((value, *earlier))[0]


def shift(value, axis, step):
    count = lax.axis_size(axis)
    return lax.ppermute(value, axis, [(i, (i + step) % count) for i in range(count)])


def own_spread(pack):
    return [pack] + [shift(pack, "sub", step) for step in range(1, lax.axis_size("sub"))]


def relay(parts, *earlier):
    pieces = []
    for part in parts:
        pieces.extend(own_spread(after(part, *earlier) if earlier else part))
    return pieces


def owner_of(band_step, sub_step):
    bands, subs = lax.axis_size("band"), lax.axis_size("sub")
    return lax.rem(lax.axis_index("band") + bands - band_step, bands) * subs + lax.rem(
        lax.axis_index("sub") + subs - sub_step, subs
    )


def load_copies(pieces, start, rows, whole, sems):
    subs = lax.axis_size("sub")
    copies = []
    for index, piece in enumerate(pieces):
        owner = owner_of(index // subs, index % subs)
        there = whole.at[pl.ds(pl.multiple_of(owner * rows, rows), rows)]
        here = piece.at[pl.ds(start, rows)]
        copies.append(pltpu.make_async_copy(here, there, sems.at[index]))
    return copies


def pack_copies(pieces, sizes, wanted, sems):
    copies = []
    for slot, (at, whole) in enumerate(wanted.items()):
        copies += load_copies(pieces, sum(sizes[:at]), sizes[at], whole, sems.at[slot])
    return copies


def pack_kernel(sets, *refs):
    sources, outs = list(refs[: sum(sets)]), refs[sum(sets) :]
    for out, amount in zip(outs, sets):
        start = 0
        for _ in range(amount):
            source = sources.pop(0)
            out[start : start + source.shape[0]] = source[...]
            start += source.shape[0]


def pack(sets):
    width = sets[0][0].shape[1]
    return pl.pallas_call(
        functools.partial(pack_kernel, [len(one) for one in sets]),
        out_shape=[
            jax.ShapeDtypeStruct((sum(weight.shape[0] for weight in one), width), jnp.bfloat16)
            for one in sets
        ],
        in_specs=[VMEM] * sum(len(one) for one in sets),
        out_specs=[VMEM] * len(sets),
        name="pack",
    )(*(weight for one in sets for weight in one))


def silu(values):
    half = 0.5 * values
    return half + half * jnp.tanh(half)


def layer_norm(values):
    average = jnp.mean(values, axis=-1, keepdims=True)
    centred = values - average
    spread_of = jnp.mean(centred * centred, axis=-1, keepdims=True)
    return centred * lax.rsqrt(spread_of + 1e-05)


def dot(a, b):
    return jnp.dot(a, b, preferred_element_type=jnp.float32)


def encode_kernel(faces, mesh_rows, sizes, target_ref, lat_ref, *refs):
    pieces, outs, (w_in, w_hid, messages, sems) = refs[: -4 - faces], refs[-4 - faces : -4], refs[-4:]
    copies = pack_copies(pieces, sizes, {0: w_in, 1: w_hid}, sems)
    for copy in copies:
        copy.start()
    for copy in copies:
        copy.wait()
    block = 256
    for start in range(0, lat_ref.shape[0], block):
        here = pl.ds(start, block)
        hidden = silu(dot(lat_ref[here], w_in[...])).astype(jnp.bfloat16)
        messages[here] = layer_norm(dot(hidden, w_hid[...])).astype(jnp.bfloat16)
    group = min(faces, 4)
    for at in range(0, faces, group):
        slots = lax.broadcasted_iota(jnp.int32, (group * mesh_rows, lat_ref.shape[0]), 0)
        chosen = jnp.where(slots + at * mesh_rows == target_ref[...], 1.0, 0.0)
        chosen = chosen.astype(jnp.bfloat16)
        sums = dot(chosen, messages[...])
        for face in range(group):
            out = outs[at + face]
            out[...] = sums[face * mesh_rows : (face + 1) * mesh_rows].astype(out.dtype)


def grid_kernel(sizes, lat_ref, *refs):
    pieces, (out_ref, w_in, w_hid, sems) = refs[:-4], refs[-4:]
    copies = pack_copies(pieces, sizes, {2: w_in, 3: w_hid}, sems)
    for copy in copies:
        copy.start()
    for copy in copies:
        copy.wait()
    block = 256
    for start in range(0, lat_ref.shape[0], block):
        here = pl.ds(start, block)
        lat = lat_ref[here]
        hidden = silu(dot(lat, w_in[...])).astype(jnp.bfloat16)
        out = lat.astype(jnp.float32) + layer_norm(dot(hidden, w_hid[...]))
        out_ref[here] = out.astype(jnp.bfloat16)


def node_kernel(sizes, faces, lat_ref, *refs):
    sums, pieces = refs[:faces], refs[faces:-5]
    head_ref, tail_ref, w_in, w_hid, sems = refs[-5:]
    width = lat_ref.shape[1]
    copies = pack_copies(pieces, sizes, {0: w_in, 1: w_hid}, sems)
    for copy in copies:
        copy.start()
    collected = sums[0][...]
    for one in sums[1:]:
        collected = collected + one[...].astype(jnp.float32)
    for copy in copies:
        copy.wait()
    lat = lat_ref[...]
    hidden = dot(lat, w_in[:width]) + dot(collected.astype(jnp.bfloat16), w_in[width:])
    hidden = silu(hidden).astype(jnp.bfloat16)
    mid = lat.astype(jnp.float32) + layer_norm(dot(hidden, w_hid[...]))
    mid = mid.astype(jnp.bfloat16)
    half = mid.shape[0] // 2
    head_ref[...] = mid[:half]
    tail_ref[...] = mid[half:]


def edge_kernel(sizes, nbr_ref, before_ref, head_ref, tail_ref, after_ref, *refs):
    pieces, (out_ref, p_in, p_hid, u_in, u_hid, sems_p, sems_u) = refs[:-7], refs[-7:]
    copies_p = pack_copies(pieces, sizes, {0: p_in, 1: p_hid}, sems_p)
    copies_u = pack_copies(pieces, sizes, {2: u_in, 3: u_hid}, sems_u)
    for copy in copies_p + copies_u:
        copy.start()
    rows, fanin = nbr_ref.shape
    width = head_ref.shape[1]
    mid = jnp.concatenate([head_ref[...], tail_ref[...]], axis=0)
    extended = jnp.concatenate([before_ref[...], mid, after_ref[...]], axis=0)
    spots = lax.broadcasted_iota(jnp.int32, (rows, extended.shape[0]), 1)
    nbr = nbr_ref[...]
    for copy in copies_p:
        copy.wait()
    receivers = dot(mid, p_in[width:])
    total = None
    group = 2 if fanin % 2 == 0 else 1
    for at in range(0, fanin, group):
        chosen = jnp.concatenate(
            [
                jnp.where(spots == nbr[:, k : k + 1], 1.0, 0.0).astype(jnp.bfloat16)
                for k in range(at, at + group)
            ],
            axis=0,
        )
        senders = dot(chosen, extended).astype(jnp.bfloat16)
        hidden = dot(senders, p_in[:width])
        hidden = (hidden.reshape(group, rows, width) + receivers[None]).reshape(group * rows, width)
        edges = layer_norm(dot(silu(hidden).astype(jnp.bfloat16), p_hid[...]))
        for k in range(group):
            one = edges[k * rows : (k + 1) * rows]
            total = one if total is None else total + one
    for copy in copies_u:
        copy.wait()
    hidden = dot(mid, u_in[:width]) + dot(total.astype(jnp.bfloat16), u_in[width:])
    hidden = silu(hidden).astype(jnp.bfloat16)
    out = mid.astype(jnp.float32) + layer_norm(dot(hidden, u_hid[...]))
    out_ref[...] = out.astype(jnp.bfloat16)


def shards(
    grid_lat,
    grid_route,
    grid_slot,
    mesh_lat,
    mesh_nbr,
    enc_w1,
    enc_w2,
    grid_w1,
    grid_w2,
    node_w1,
    node_w2,
    proc_w1,
    proc_w2,
    upd_w1,
    upd_w2,
):
    grid_rows, width = grid_lat.shape
    mesh_rows = mesh_lat.shape[0]
    faces = lax.axis_size("face")
    bands = lax.axis_size("band")
    count = bands * lax.axis_size("sub")
    f32, bf16 = jnp.float32, jnp.bfloat16

    def matrix(weight):
        return pltpu.VMEM((weight.shape[0] * count, weight.shape[1]), bf16)

    def sems(*shape):
        return pltpu.SemaphoreType.DMA(shape)

    def cost(rows, depth):
        return pl.CostEstimate(
            flops=2 * rows * depth * width,
            bytes_accessed=2 * (rows + depth) * width,
            transcendentals=rows * width,
        )

    sets = ((node_w1, node_w2, grid_w1, grid_w2), (proc_w1, proc_w2, upd_w1, upd_w2))
    sizes = [[weight.shape[0] for weight in one] for one in sets]
    enc_pack, early, late = pack([(enc_w1, enc_w2), *sets])
    enc_far = [shift(enc_pack, "band", step) for step in range(1, bands)]
    enc_near = own_spread(enc_pack)
    enc_all = enc_near + relay(enc_far)
    early_sent = after(early, *enc_far)
    early_far = [shift(early_sent, "band", step) for step in range(1, bands)]
    early_near, late_near = own_spread(early), own_spread(late)

    me = lax.axis_index("face")
    distance = lax.rem(grid_route[:, 0] - me + faces, faces)
    targets = (distance * mesh_rows + grid_slot).reshape(1, grid_rows)

    block = (mesh_rows, width)
    sums = pl.pallas_call(
        functools.partial(
            encode_kernel, faces, mesh_rows, [enc_w1.shape[0], enc_w2.shape[0]]
        ),
        out_shape=[
            jax.ShapeDtypeStruct(block, bf16 if step else f32) for step in range(faces)
        ],
        in_specs=[VMEM, VMEM] + [ANY] * len(enc_all),
        out_specs=[VMEM] * faces,
        scratch_shapes=[
            matrix(enc_w1),
            matrix(enc_w2),
            pltpu.VMEM((grid_rows, width), bf16),
            sems(2, count),
        ],
        compiler_params=pltpu.CompilerParams(vmem_limit_bytes=32 * MIB),
        cost_estimate=cost(grid_rows, 3 * width),
        name="encode",
    )(targets, after(grid_lat, *early_near, *late_near), *enc_all)
    late_sent = after(late, sums[0])
    late_far = [shift(late_sent, "band", step) for step in range(1, bands)]
    arrived = [sums[0]] + [shift(sums[step], "face", step) for step in range(1, faces)]

    early_all = early_near + relay(early_far, *arrived[1:])
    grid_out = pl.pallas_call(
        functools.partial(grid_kernel, sizes[0]),
        out_shape=jax.ShapeDtypeStruct(grid_lat.shape, bf16),
        in_specs=[VMEM] + [ANY] * len(early_all),
        out_specs=VMEM,
        scratch_shapes=[matrix(grid_w1), matrix(grid_w2), sems(2, count)],
        compiler_params=pltpu.CompilerParams(vmem_limit_bytes=32 * MIB),
        cost_estimate=cost(grid_rows, 2 * width),
        name="grid_update",
    )(grid_lat, *early_all)

    half = (mesh_rows // 2, width)
    head, tail = pl.pallas_call(
        functools.partial(node_kernel, sizes[0], faces),
        out_shape=[jax.ShapeDtypeStruct(half, bf16)] * 2,
        in_specs=[VMEM] * (1 + faces) + [ANY] * len(early_all),
        out_specs=[VMEM] * 2,
        scratch_shapes=[matrix(node_w1), matrix(node_w2), sems(2, count)],
        compiler_params=pltpu.CompilerParams(vmem_limit_bytes=32 * MIB),
        cost_estimate=cost(mesh_rows, 3 * width),
        name="node_update",
    )(mesh_lat, *arrived, *early_all)

    before = shift(tail, "face", 1)
    behind = shift(head, "face", faces - 1)
    late_all = late_near + relay(late_far, head)
    mesh_out = pl.pallas_call(
        functools.partial(edge_kernel, sizes[1]),
        out_shape=jax.ShapeDtypeStruct(mesh_lat.shape, bf16),
        in_specs=[VMEM] * 5 + [ANY] * len(late_all),
        out_specs=VMEM,
        scratch_shapes=[
            matrix(proc_w1),
            matrix(proc_w2),
            matrix(upd_w1),
            matrix(upd_w2),
            sems(2, count),
            sems(2, count),
        ],
        compiler_params=pltpu.CompilerParams(vmem_limit_bytes=32 * MIB),
        cost_estimate=cost(mesh_rows * mesh_nbr.shape[1], 3 * width),
        name="edge_update",
    )(mesh_nbr, before, head, tail, behind, *late_all)
    return (grid_out, mesh_out)


def solution(mesh):
    rows = ("groups", "face", "band", "sub")
    placed = (
        P(rows, None),
        P(rows, None),
        P(rows),
        P(rows, None),
        P(rows, None),
    ) + (P(("band", "sub"), None),) * 10
    return jax.shard_map(
        shards,
        mesh=mesh,
        in_specs=placed,
        out_specs=(P(rows, None), P(rows, None)),
        check_vma=False,
    )
```

```python
import functools

import jax
import jax.numpy as jnp
from jax import lax
from jax.experimental import pallas as pl
from jax.experimental.pallas import tpu as pltpu
from jax.sharding import PartitionSpec as P

MIB = 1 << 20
ANY = pl.BlockSpec(memory_space=pl.ANY)
VMEM = pl.BlockSpec(memory_space=pltpu.VMEM)


def after(value, *earlier):
    return lax.optimization_barrier((value, *earlier))[0]


def shift(value, axis, step):
    count = lax.axis_size(axis)
    return lax.ppermute(value, axis, [(i, (i + step) % count) for i in range(count)])


def own_spread(pack):
    return [pack] + [shift(pack, "sub", step) for step in range(1, lax.axis_size("sub"))]


def relay(parts, *earlier):
    pieces = []
    for part in parts:
        pieces.extend(own_spread(after(part, *earlier) if earlier else part))
    return pieces


def owner_of(band_step, sub_step):
    bands, subs = lax.axis_size("band"), lax.axis_size("sub")
    return lax.rem(lax.axis_index("band") + bands - band_step, bands) * subs + lax.rem(
        lax.axis_index("sub") + subs - sub_step, subs
    )


def load_copies(pieces, start, rows, whole, sems):
    subs = lax.axis_size("sub")
    copies = []
    for index, piece in enumerate(pieces):
        owner = owner_of(index // subs, index % subs)
        there = whole.at[pl.ds(pl.multiple_of(owner * rows, rows), rows)]
        here = piece.at[pl.ds(start, rows)]
        copies.append(pltpu.make_async_copy(here, there, sems.at[index]))
    return copies


def pack_copies(pieces, sizes, wanted, sems):
    copies = []
    for slot, (at, whole) in enumerate(wanted.items()):
        copies += load_copies(pieces, sum(sizes[:at]), sizes[at], whole, sems.at[slot])
    return copies


def pack_kernel(sets, *refs):
    sources, outs = list(refs[: sum(sets)]), refs[sum(sets) :]
    for out, amount in zip(outs, sets):
        start = 0
        for _ in range(amount):
            source = sources.pop(0)
            out[start : start + source.shape[0]] = source[...]
            start += source.shape[0]


def pack(sets):
    width = sets[0][0].shape[1]
    return pl.pallas_call(
        functools.partial(pack_kernel, [len(one) for one in sets]),
        out_shape=[
            jax.ShapeDtypeStruct((sum(weight.shape[0] for weight in one), width), jnp.bfloat16)
            for one in sets
        ],
        in_specs=[VMEM] * sum(len(one) for one in sets),
        out_specs=[VMEM] * len(sets),
        name="pack",
    )(*(weight for one in sets for weight in one))


def silu(values):
    half = 0.5 * values
    return half + half * jnp.tanh(half)


def layer_norm(values):
    average = jnp.mean(values, axis=-1, keepdims=True)
    centred = values - average
    spread_of = jnp.mean(centred * centred, axis=-1, keepdims=True)
    return centred * lax.rsqrt(spread_of + 1e-05)


def dot(a, b):
    return jnp.dot(a, b, preferred_element_type=jnp.float32)


def encode_kernel(count, faces, mesh_rows, target_ref, lat_ref, *refs):
    in_pieces, hid_pieces = refs[:count], refs[count : 2 * count]
    outs = refs[2 * count : 2 * count + faces]
    w_in, w_hid, messages, sems = refs[2 * count + faces :]
    rows = w_in.shape[0] // count
    copies = load_copies(in_pieces, 0, rows, w_in, sems.at[0])
    copies += load_copies(hid_pieces, 0, rows, w_hid, sems.at[1])
    for copy in copies:
        copy.start()
    for copy in copies:
        copy.wait()
    block = 256
    for start in range(0, lat_ref.shape[0], block):
        here = pl.ds(start, block)
        hidden = silu(dot(lat_ref[here], w_in[...])).astype(jnp.bfloat16)
        messages[here] = layer_norm(dot(hidden, w_hid[...])).astype(jnp.bfloat16)
    group = min(faces, 4)
    for at in range(0, faces, group):
        slots = lax.broadcasted_iota(jnp.int32, (group * mesh_rows, lat_ref.shape[0]), 0)
        chosen = jnp.where(slots + at * mesh_rows == target_ref[...], 1.0, 0.0)
        chosen = chosen.astype(jnp.bfloat16)
        sums = dot(chosen, messages[...])
        for face in range(group):
            out = outs[at + face]
            out[...] = sums[face * mesh_rows : (face + 1) * mesh_rows].astype(out.dtype)


def grid_kernel(sizes, lat_ref, *refs):
    pieces, (out_ref, w_in, w_hid, sems) = refs[:-4], refs[-4:]
    copies = pack_copies(pieces, sizes, {2: w_in, 3: w_hid}, sems)
    for copy in copies:
        copy.start()
    for copy in copies:
        copy.wait()
    block = 256
    for start in range(0, lat_ref.shape[0], block):
        here = pl.ds(start, block)
        lat = lat_ref[here]
        hidden = silu(dot(lat, w_in[...])).astype(jnp.bfloat16)
        out = lat.astype(jnp.float32) + layer_norm(dot(hidden, w_hid[...]))
        out_ref[here] = out.astype(jnp.bfloat16)


def node_kernel(sizes, faces, lat_ref, *refs):
    sums, pieces = refs[:faces], refs[faces:-5]
    head_ref, tail_ref, w_in, w_hid, sems = refs[-5:]
    width = lat_ref.shape[1]
    copies = pack_copies(pieces, sizes, {0: w_in, 1: w_hid}, sems)
    for copy in copies:
        copy.start()
    collected = sums[0][...]
    for one in sums[1:]:
        collected = collected + one[...].astype(jnp.float32)
    for copy in copies:
        copy.wait()
    lat = lat_ref[...]
    hidden = dot(lat, w_in[:width]) + dot(collected.astype(jnp.bfloat16), w_in[width:])
    hidden = silu(hidden).astype(jnp.bfloat16)
    mid = lat.astype(jnp.float32) + layer_norm(dot(hidden, w_hid[...]))
    mid = mid.astype(jnp.bfloat16)
    half = mid.shape[0] // 2
    head_ref[...] = mid[:half]
    tail_ref[...] = mid[half:]


def edge_kernel(sizes, nbr_ref, before_ref, head_ref, tail_ref, after_ref, *refs):
    pieces, (out_ref, p_in, p_hid, u_in, u_hid, sems_p, sems_u) = refs[:-7], refs[-7:]
    copies_p = pack_copies(pieces, sizes, {0: p_in, 1: p_hid}, sems_p)
    copies_u = pack_copies(pieces, sizes, {2: u_in, 3: u_hid}, sems_u)
    for copy in copies_p + copies_u:
        copy.start()
    rows, fanin = nbr_ref.shape
    width = head_ref.shape[1]
    mid = jnp.concatenate([head_ref[...], tail_ref[...]], axis=0)
    extended = jnp.concatenate([before_ref[...], mid, after_ref[...]], axis=0)
    spots = lax.broadcasted_iota(jnp.int32, (rows, extended.shape[0]), 1)
    nbr = nbr_ref[...]
    for copy in copies_p:
        copy.wait()
    receivers = dot(mid, p_in[width:])
    total = None
    group = 2 if fanin % 2 == 0 else 1
    for at in range(0, fanin, group):
        chosen = jnp.concatenate(
            [
                jnp.where(spots == nbr[:, k : k + 1], 1.0, 0.0).astype(jnp.bfloat16)
                for k in range(at, at + group)
            ],
            axis=0,
        )
        senders = dot(chosen, extended).astype(jnp.bfloat16)
        hidden = dot(senders, p_in[:width])
        hidden = (hidden.reshape(group, rows, width) + receivers[None]).reshape(group * rows, width)
        edges = layer_norm(dot(silu(hidden).astype(jnp.bfloat16), p_hid[...]))
        for k in range(group):
            one = edges[k * rows : (k + 1) * rows]
            total = one if total is None else total + one
    for copy in copies_u:
        copy.wait()
    hidden = dot(mid, u_in[:width]) + dot(total.astype(jnp.bfloat16), u_in[width:])
    hidden = silu(hidden).astype(jnp.bfloat16)
    out = mid.astype(jnp.float32) + layer_norm(dot(hidden, u_hid[...]))
    out_ref[...] = out.astype(jnp.bfloat16)


def shards(
    grid_lat,
    grid_route,
    grid_slot,
    mesh_lat,
    mesh_nbr,
    enc_w1,
    enc_w2,
    grid_w1,
    grid_w2,
    node_w1,
    node_w2,
    proc_w1,
    proc_w2,
    upd_w1,
    upd_w2,
):
    grid_rows, width = grid_lat.shape
    mesh_rows = mesh_lat.shape[0]
    faces = lax.axis_size("face")
    bands = lax.axis_size("band")
    count = bands * lax.axis_size("sub")
    f32, bf16 = jnp.float32, jnp.bfloat16

    def matrix(weight):
        return pltpu.VMEM((weight.shape[0] * count, weight.shape[1]), bf16)

    def sems(*shape):
        return pltpu.SemaphoreType.DMA(shape)

    def cost(rows, depth):
        return pl.CostEstimate(
            flops=2 * rows * depth * width,
            bytes_accessed=2 * (rows + depth) * width,
            transcendentals=rows * width,
        )

    sets = ((node_w1, node_w2, grid_w1, grid_w2), (proc_w1, proc_w2, upd_w1, upd_w2))
    sizes = [[weight.shape[0] for weight in one] for one in sets]
    enc_far = [[shift(one, "band", step) for step in range(1, bands)] for one in (enc_w1, enc_w2)]
    enc_all = [
        own_spread(one) + relay(far) for one, far in zip((enc_w1, enc_w2), enc_far)
    ]
    early, late = pack(sets)
    early_sent = after(early, *enc_far[0], *enc_far[1])
    early_far = [shift(early_sent, "band", step) for step in range(1, bands)]
    early_near, late_near = own_spread(early), own_spread(late)

    me = lax.axis_index("face")
    distance = lax.rem(grid_route[:, 0] - me + faces, faces)
    targets = (distance * mesh_rows + grid_slot).reshape(1, grid_rows)

    block = (mesh_rows, width)
    sums = pl.pallas_call(
        functools.partial(encode_kernel, count, faces, mesh_rows),
        out_shape=[
            jax.ShapeDtypeStruct(block, bf16 if step else f32) for step in range(faces)
        ],
        in_specs=[VMEM, VMEM] + [ANY] * (2 * count),
        out_specs=[VMEM] * faces,
        scratch_shapes=[
            matrix(enc_w1),
            matrix(enc_w2),
            pltpu.VMEM((grid_rows, width), bf16),
            sems(2, count),
        ],
        compiler_params=pltpu.CompilerParams(vmem_limit_bytes=32 * MIB),
        cost_estimate=cost(grid_rows, 3 * width),
        name="encode",
    )(targets, grid_lat, *enc_all[0], *enc_all[1])
    late_sent = after(late, sums[0])
    late_far = [shift(late_sent, "band", step) for step in range(1, bands)]
    arrived = [sums[0]] + [shift(sums[step], "face", step) for step in range(1, faces)]

    early_all = early_near + relay(early_far, *arrived[1:])
    grid_out = pl.pallas_call(
        functools.partial(grid_kernel, sizes[0]),
        out_shape=jax.ShapeDtypeStruct(grid_lat.shape, bf16),
        in_specs=[VMEM] + [ANY] * len(early_all),
        out_specs=VMEM,
        scratch_shapes=[matrix(grid_w1), matrix(grid_w2), sems(2, count)],
        compiler_params=pltpu.CompilerParams(vmem_limit_bytes=32 * MIB),
        cost_estimate=cost(grid_rows, 2 * width),
        name="grid_update",
    )(grid_lat, *early_all)

    half = (mesh_rows // 2, width)
    head, tail = pl.pallas_call(
        functools.partial(node_kernel, sizes[0], faces),
        out_shape=[jax.ShapeDtypeStruct(half, bf16)] * 2,
        in_specs=[VMEM] * (1 + faces) + [ANY] * len(early_all),
        out_specs=[VMEM] * 2,
        scratch_shapes=[matrix(node_w1), matrix(node_w2), sems(2, count)],
        compiler_params=pltpu.CompilerParams(vmem_limit_bytes=32 * MIB),
        cost_estimate=cost(mesh_rows, 3 * width),
        name="node_update",
    )(mesh_lat, *arrived, *early_all)

    before = shift(tail, "face", 1)
    behind = shift(head, "face", faces - 1)
    late_all = late_near + relay(late_far, head, grid_out)
    mesh_out = pl.pallas_call(
        functools.partial(edge_kernel, sizes[1]),
        out_shape=jax.ShapeDtypeStruct(mesh_lat.shape, bf16),
        in_specs=[VMEM] * 5 + [ANY] * len(late_all),
        out_specs=VMEM,
        scratch_shapes=[
            matrix(proc_w1),
            matrix(proc_w2),
            matrix(upd_w1),
            matrix(upd_w2),
            sems(2, count),
            sems(2, count),
        ],
        compiler_params=pltpu.CompilerParams(vmem_limit_bytes=32 * MIB),
        cost_estimate=cost(mesh_rows * mesh_nbr.shape[1], 3 * width),
        name="edge_update",
    )(mesh_nbr, before, head, tail, behind, *late_all)
    return (grid_out, mesh_out)


def solution(mesh):
    rows = ("groups", "face", "band", "sub")
    placed = (
        P(rows, None),
        P(rows, None),
        P(rows),
        P(rows, None),
        P(rows, None),
    ) + (P(("band", "sub"), None),) * 10
    return jax.shard_map(
        shards,
        mesh=mesh,
        in_specs=placed,
        out_specs=(P(rows, None), P(rows, None)),
        check_vma=False,
    )
```

```python
import functools

import jax
import jax.numpy as jnp
from jax import lax
from jax.experimental import pallas as pl
from jax.experimental.pallas import tpu as pltpu
from jax.sharding import PartitionSpec as P

MIB = 1 << 20
ANY = pl.BlockSpec(memory_space=pl.ANY)
VMEM = pl.BlockSpec(memory_space=pltpu.VMEM)


def after(value, *earlier):
    return lax.optimization_barrier((value, *earlier))[0]


def shift(value, axis, step):
    count = lax.axis_size(axis)
    return lax.ppermute(value, axis, [(i, (i + step) % count) for i in range(count)])


def own_spread(pack):
    return [pack] + [shift(pack, "sub", step) for step in range(1, lax.axis_size("sub"))]


def relay(parts, *earlier):
    pieces = []
    for part in parts:
        pieces.extend(own_spread(after(part, *earlier) if earlier else part))
    return pieces


def owner_of(band_step, sub_step):
    bands, subs = lax.axis_size("band"), lax.axis_size("sub")
    return lax.rem(lax.axis_index("band") + bands - band_step, bands) * subs + lax.rem(
        lax.axis_index("sub") + subs - sub_step, subs
    )


def load_copies(pieces, starts, rows, whole, sems):
    subs = lax.axis_size("sub")
    copies = []
    for index, (piece, start) in enumerate(zip(pieces, starts)):
        owner = owner_of(index // subs, index % subs)
        there = whole.at[pl.ds(pl.multiple_of(owner * rows, rows), rows)]
        here = piece.at[pl.ds(start, rows)]
        copies.append(pltpu.make_async_copy(here, there, sems.at[index]))
    return copies


def pack_copies(pieces, base, sizes, wanted, sems):
    subs = lax.axis_size("sub")
    copies = []
    for slot, (at, whole) in enumerate(wanted.items()):
        start = sum(sizes[:at])
        starts = [base + start] * subs + [start] * (len(pieces) - subs)
        copies += load_copies(pieces, starts, sizes[at], whole, sems.at[slot])
    return copies


def pack_kernel(sets, *refs):
    sources, outs, everything = list(refs[: sum(sets)]), refs[sum(sets) : -1], refs[-1]
    whole_start = 0
    for out, amount in zip(outs, sets):
        start = 0
        for _ in range(amount):
            values = sources.pop(0)[...]
            rows = values.shape[0]
            out[start : start + rows] = values
            everything[whole_start : whole_start + rows] = values
            start, whole_start = start + rows, whole_start + rows


def pack(sets):
    width = sets[0][0].shape[1]
    rows = [sum(weight.shape[0] for weight in one) for one in sets]
    return pl.pallas_call(
        functools.partial(pack_kernel, [len(one) for one in sets]),
        out_shape=[jax.ShapeDtypeStruct((size, width), jnp.bfloat16) for size in rows + [sum(rows)]],
        in_specs=[VMEM] * sum(len(one) for one in sets),
        out_specs=[VMEM] * (len(sets) + 1),
        name="pack",
    )(*(weight for one in sets for weight in one))


def silu(values):
    half = 0.5 * values
    return half + half * jnp.tanh(half)


def layer_norm(values):
    average = jnp.mean(values, axis=-1, keepdims=True)
    centred = values - average
    spread_of = jnp.mean(centred * centred, axis=-1, keepdims=True)
    return centred * lax.rsqrt(spread_of + 1e-05)


def dot(a, b):
    return jnp.dot(a, b, preferred_element_type=jnp.float32)


def encode_kernel(count, target_ref, lat_ref, *refs):
    in_pieces, hid_pieces = refs[:count], refs[count : 2 * count]
    out_ref, w_in, w_hid, messages, sems = refs[2 * count :]
    rows = w_in.shape[0] // count
    copies = load_copies(in_pieces, [0] * count, rows, w_in, sems.at[0])
    copies += load_copies(hid_pieces, [0] * count, rows, w_hid, sems.at[1])
    for copy in copies:
        copy.start()
    for copy in copies:
        copy.wait()
    block = 256
    for start in range(0, lat_ref.shape[0], block):
        here = pl.ds(start, block)
        hidden = silu(dot(lat_ref[here], w_in[...])).astype(jnp.bfloat16)
        messages[here] = layer_norm(dot(hidden, w_hid[...])).astype(jnp.bfloat16)
    slots = out_ref.shape[0]
    block = min(slots, 512)
    for start in range(0, slots, block):
        here = lax.broadcasted_iota(jnp.int32, (block, lat_ref.shape[0]), 0) + start
        chosen = jnp.where(here == target_ref[...], 1.0, 0.0).astype(jnp.bfloat16)
        out_ref[pl.ds(start, block)] = dot(chosen, messages[...]).astype(out_ref.dtype)


def grid_kernel(base, sizes, lat_ref, *refs):
    pieces, (out_ref, w_in, w_hid, sems) = refs[:-4], refs[-4:]
    copies = pack_copies(pieces, base, sizes, {0: w_in, 1: w_hid}, sems)
    for copy in copies:
        copy.start()
    for copy in copies:
        copy.wait()
    block = 256
    for start in range(0, lat_ref.shape[0], block):
        here = pl.ds(start, block)
        lat = lat_ref[here]
        hidden = silu(dot(lat, w_in[...])).astype(jnp.bfloat16)
        out = lat.astype(jnp.float32) + layer_norm(dot(hidden, w_hid[...]))
        out_ref[here] = out.astype(jnp.bfloat16)


def node_kernel(base, sizes, lat_ref, sums_ref, *refs):
    pieces = refs[:-5]
    head_ref, tail_ref, w_in, w_hid, sems = refs[-5:]
    width = lat_ref.shape[1]
    copies = pack_copies(pieces, base, sizes, {0: w_in, 1: w_hid}, sems)
    for copy in copies:
        copy.start()
    rows = lat_ref.shape[0]
    collected = sums_ref[:rows].astype(jnp.float32)
    for start in range(rows, sums_ref.shape[0], rows):
        collected = collected + sums_ref[start : start + rows].astype(jnp.float32)
    for copy in copies:
        copy.wait()
    lat = lat_ref[...]
    hidden = dot(lat, w_in[:width]) + dot(collected.astype(jnp.bfloat16), w_in[width:])
    hidden = silu(hidden).astype(jnp.bfloat16)
    mid = lat.astype(jnp.float32) + layer_norm(dot(hidden, w_hid[...]))
    mid = mid.astype(jnp.bfloat16)
    half = mid.shape[0] // 2
    head_ref[...] = mid[:half]
    tail_ref[...] = mid[half:]


def edge_kernel(base, sizes, nbr_ref, before_ref, head_ref, tail_ref, after_ref, *refs):
    pieces, (out_ref, p_in, p_hid, u_in, u_hid, sems_p, sems_u) = refs[:-7], refs[-7:]
    copies_p = pack_copies(pieces, base, sizes, {0: p_in, 1: p_hid}, sems_p)
    copies_u = pack_copies(pieces, base, sizes, {2: u_in, 3: u_hid}, sems_u)
    for copy in copies_p + copies_u:
        copy.start()
    rows, fanin = nbr_ref.shape
    width = head_ref.shape[1]
    mid = jnp.concatenate([head_ref[...], tail_ref[...]], axis=0)
    extended = jnp.concatenate([before_ref[...], mid, after_ref[...]], axis=0)
    spots = lax.broadcasted_iota(jnp.int32, (rows, extended.shape[0]), 1)
    nbr = nbr_ref[...]
    for copy in copies_p:
        copy.wait()
    receivers = dot(mid, p_in[width:])
    total = None
    group = 2 if fanin % 2 == 0 else 1
    for at in range(0, fanin, group):
        chosen = jnp.concatenate(
            [
                jnp.where(spots == nbr[:, k : k + 1], 1.0, 0.0).astype(jnp.bfloat16)
                for k in range(at, at + group)
            ],
            axis=0,
        )
        senders = dot(chosen, extended).astype(jnp.bfloat16)
        hidden = dot(senders, p_in[:width])
        hidden = (hidden.reshape(group, rows, width) + receivers[None]).reshape(group * rows, width)
        edges = layer_norm(dot(silu(hidden).astype(jnp.bfloat16), p_hid[...]))
        for k in range(group):
            one = edges[k * rows : (k + 1) * rows]
            total = one if total is None else total + one
    for copy in copies_u:
        copy.wait()
    hidden = dot(mid, u_in[:width]) + dot(total.astype(jnp.bfloat16), u_in[width:])
    hidden = silu(hidden).astype(jnp.bfloat16)
    out = mid.astype(jnp.float32) + layer_norm(dot(hidden, u_hid[...]))
    out_ref[...] = out.astype(jnp.bfloat16)


def shards(
    grid_lat,
    grid_route,
    grid_slot,
    mesh_lat,
    mesh_nbr,
    enc_w1,
    enc_w2,
    grid_w1,
    grid_w2,
    node_w1,
    node_w2,
    proc_w1,
    proc_w2,
    upd_w1,
    upd_w2,
):
    grid_rows, width = grid_lat.shape
    mesh_rows = mesh_lat.shape[0]
    faces = lax.axis_size("face")
    bands = lax.axis_size("band")
    count = bands * lax.axis_size("sub")
    bf16 = jnp.bfloat16

    def matrix(weight):
        return pltpu.VMEM((weight.shape[0] * count, weight.shape[1]), bf16)

    def sems(*shape):
        return pltpu.SemaphoreType.DMA(shape)

    def cost(rows, depth):
        return pl.CostEstimate(
            flops=2 * rows * depth * width,
            bytes_accessed=2 * (rows + depth) * width,
            transcendentals=rows * width,
        )

    sets = ((node_w1, node_w2), (grid_w1, grid_w2), (proc_w1, proc_w2, upd_w1, upd_w2))
    sizes = [[weight.shape[0] for weight in one] for one in sets]
    bases = [sum(sum(one) for one in sizes[:at]) for at in range(len(sets))]
    enc_far = [[shift(one, "band", step) for step in range(1, bands)] for one in (enc_w1, enc_w2)]
    enc_all = [
        own_spread(one) + relay(far) for one, far in zip((enc_w1, enc_w2), enc_far)
    ]
    node, grid, late, everything = pack(sets)
    near = own_spread(everything)
    node_sent = after(node, *enc_far[0])
    node_far = [shift(node_sent, "band", step) for step in range(1, bands)]
    grid_sent = after(grid, *enc_far[1])
    grid_far = [shift(grid_sent, "band", step) for step in range(1, bands)]
    late_sent = after(late, enc_all[0][-1], *enc_far[1])
    late_far = [shift(late_sent, "band", step) for step in range(1, bands)]

    targets = (grid_route[:, 0] * mesh_rows + grid_slot).reshape(1, grid_rows)
    sums = pl.pallas_call(
        functools.partial(encode_kernel, count),
        out_shape=jax.ShapeDtypeStruct((faces * mesh_rows, width), bf16),
        in_specs=[VMEM, VMEM] + [ANY] * (2 * count),
        out_specs=VMEM,
        scratch_shapes=[
            matrix(enc_w1),
            matrix(enc_w2),
            pltpu.VMEM((grid_rows, width), bf16),
            sems(2, count),
        ],
        compiler_params=pltpu.CompilerParams(vmem_limit_bytes=32 * MIB),
        cost_estimate=cost(grid_rows, 3 * width),
        name="encode",
    )(targets, grid_lat, *enc_all[0], *enc_all[1])
    node_all = near + relay(node_far, sums)
    arrived = lax.all_to_all(sums, "face", split_axis=0, concat_axis=0, tiled=True)

    grid_all = near + relay(grid_far, arrived)
    grid_out = pl.pallas_call(
        functools.partial(grid_kernel, bases[1], sizes[1]),
        out_shape=jax.ShapeDtypeStruct(grid_lat.shape, bf16),
        in_specs=[VMEM] + [ANY] * len(grid_all),
        out_specs=VMEM,
        scratch_shapes=[matrix(grid_w1), matrix(grid_w2), sems(2, count)],
        compiler_params=pltpu.CompilerParams(vmem_limit_bytes=32 * MIB),
        cost_estimate=cost(grid_rows, 2 * width),
        name="grid_update",
    )(grid_lat, *grid_all)

    half = (mesh_rows // 2, width)
    head, tail = pl.pallas_call(
        functools.partial(node_kernel, bases[0], sizes[0]),
        out_shape=[jax.ShapeDtypeStruct(half, bf16)] * 2,
        in_specs=[VMEM] * 2 + [ANY] * len(node_all),
        out_specs=[VMEM] * 2,
        scratch_shapes=[matrix(node_w1), matrix(node_w2), sems(2, count)],
        compiler_params=pltpu.CompilerParams(vmem_limit_bytes=32 * MIB),
        cost_estimate=cost(mesh_rows, 3 * width),
        name="node_update",
    )(mesh_lat, arrived, *node_all)

    before = shift(tail, "face", 1)
    behind = shift(head, "face", faces - 1)
    late_all = near + relay(late_far, before, behind, grid_out)
    mesh_out = pl.pallas_call(
        functools.partial(edge_kernel, bases[2], sizes[2]),
        out_shape=jax.ShapeDtypeStruct(mesh_lat.shape, bf16),
        in_specs=[VMEM] * 5 + [ANY] * len(late_all),
        out_specs=VMEM,
        scratch_shapes=[
            matrix(proc_w1),
            matrix(proc_w2),
            matrix(upd_w1),
            matrix(upd_w2),
            sems(2, count),
            sems(2, count),
        ],
        compiler_params=pltpu.CompilerParams(vmem_limit_bytes=32 * MIB),
        cost_estimate=cost(mesh_rows * mesh_nbr.shape[1], 3 * width),
        name="edge_update",
    )(mesh_nbr, before, head, tail, behind, *late_all)
    return (grid_out, mesh_out)


def solution(mesh):
    rows = ("groups", "face", "band", "sub")
    placed = (
        P(rows, None),
        P(rows, None),
        P(rows),
        P(rows, None),
        P(rows, None),
    ) + (P(("band", "sub"), None),) * 10
    return jax.shard_map(
        shards,
        mesh=mesh,
        in_specs=placed,
        out_specs=(P(rows, None), P(rows, None)),
        check_vma=False,
    )
```

```python
import functools

import jax
import jax.numpy as jnp
from jax import lax
from jax.experimental import pallas as pl
from jax.experimental.pallas import tpu as pltpu
from jax.sharding import PartitionSpec as P

MIB = 1 << 20
VMEM = pl.BlockSpec(memory_space=pltpu.VMEM)


def after(value, *earlier):
    return lax.optimization_barrier((value, *earlier))[0]


def shift(value, axis, step):
    count = lax.axis_size(axis)
    return lax.ppermute(value, axis, [(i, (i + step) % count) for i in range(count)])


def distances(faces):
    if faces & (faces - 1):
        return list(range(faces))
    return [0] + sorted(range(1, faces), key=lambda step: (step == 1, step))


def face_at(faces, step, me):
    return (me + step) % faces if faces & (faces - 1) else me ^ step


def to_face(value, step):
    faces = lax.axis_size("face")
    return lax.ppermute(value, "face", [(i, face_at(faces, step, i)) for i in range(faces)])


def own_spread(pack):
    return [pack] + [shift(pack, "sub", step) for step in range(1, lax.axis_size("sub"))]


def relay(parts, *earlier):
    pieces = []
    for part in parts:
        pieces.extend(own_spread(after(part, *earlier) if earlier else part))
    return pieces


def owner_of(band_step, sub_step):
    bands, subs = lax.axis_size("band"), lax.axis_size("sub")
    return lax.rem(lax.axis_index("band") + bands - band_step, bands) * subs + lax.rem(
        lax.axis_index("sub") + subs - sub_step, subs
    )


def place(pieces, start, rows, whole):
    subs = lax.axis_size("sub")
    for index, piece in enumerate(pieces):
        owner = owner_of(index // subs, index % subs)
        whole[pl.ds(pl.multiple_of(owner * rows, rows), rows)] = piece[start : start + rows]


def unpack(pieces, sizes, wanted):
    for at, whole in wanted.items():
        place(pieces, sum(sizes[:at]), sizes[at], whole)


def pack_kernel(sets, *refs):
    sources, outs = list(refs[: sum(sets)]), refs[sum(sets) :]
    for out, amount in zip(outs, sets):
        start = 0
        for _ in range(amount):
            source = sources.pop(0)
            out[start : start + source.shape[0]] = source[...]
            start += source.shape[0]


def pack(sets):
    width = sets[0][0].shape[1]
    return pl.pallas_call(
        functools.partial(pack_kernel, [len(one) for one in sets]),
        out_shape=[
            jax.ShapeDtypeStruct((sum(weight.shape[0] for weight in one), width), jnp.bfloat16)
            for one in sets
        ],
        in_specs=[VMEM] * sum(len(one) for one in sets),
        out_specs=[VMEM] * len(sets),
        name="pack",
    )(*(weight for one in sets for weight in one))


def silu(values):
    half = 0.5 * values
    return half + half * jnp.tanh(half)


def layer_norm(values):
    average = jnp.mean(values, axis=-1, keepdims=True)
    centred = values - average
    spread_of = jnp.mean(centred * centred, axis=-1, keepdims=True)
    return centred * lax.rsqrt(spread_of + 1e-05)


def dot(a, b):
    return jnp.dot(a, b, preferred_element_type=jnp.float32)


def encode_kernel(count, faces, mesh_rows, target_ref, lat_ref, *refs):
    in_pieces, hid_pieces = refs[:count], refs[count : 2 * count]
    outs = refs[2 * count : 2 * count + faces]
    w_in, w_hid, messages = refs[2 * count + faces :]
    rows = w_in.shape[0] // count
    place(in_pieces, 0, rows, w_in)
    place(hid_pieces, 0, rows, w_hid)
    block = 256
    for start in range(0, lat_ref.shape[0], block):
        here = pl.ds(start, block)
        hidden = silu(dot(lat_ref[here], w_in[...])).astype(jnp.bfloat16)
        messages[here] = layer_norm(dot(hidden, w_hid[...])).astype(jnp.bfloat16)
    group = min(faces, 4)
    for at in range(0, faces, group):
        slots = lax.broadcasted_iota(jnp.int32, (group * mesh_rows, lat_ref.shape[0]), 0)
        chosen = jnp.where(slots + at * mesh_rows == target_ref[...], 1.0, 0.0)
        chosen = chosen.astype(jnp.bfloat16)
        sums = dot(chosen, messages[...])
        for face in range(group):
            out = outs[at + face]
            out[...] = sums[face * mesh_rows : (face + 1) * mesh_rows].astype(out.dtype)


def grid_kernel(sizes, lat_ref, *refs):
    pieces, (out_ref, w_in, w_hid) = refs[:-3], refs[-3:]
    unpack(pieces, sizes, {2: w_in, 3: w_hid})
    block = 256
    for start in range(0, lat_ref.shape[0], block):
        here = pl.ds(start, block)
        lat = lat_ref[here]
        hidden = silu(dot(lat, w_in[...])).astype(jnp.bfloat16)
        out = lat.astype(jnp.float32) + layer_norm(dot(hidden, w_hid[...]))
        out_ref[here] = out.astype(jnp.bfloat16)


def node_kernel(sizes, faces, lat_ref, *refs):
    sums, pieces = refs[:faces], refs[faces:-4]
    head_ref, tail_ref, w_in, w_hid = refs[-4:]
    width = lat_ref.shape[1]
    unpack(pieces, sizes, {0: w_in, 1: w_hid})
    collected = sums[0][...]
    for one in sums[1:]:
        collected = collected + one[...].astype(jnp.float32)
    lat = lat_ref[...]
    hidden = dot(lat, w_in[:width]) + dot(collected.astype(jnp.bfloat16), w_in[width:])
    hidden = silu(hidden).astype(jnp.bfloat16)
    mid = lat.astype(jnp.float32) + layer_norm(dot(hidden, w_hid[...]))
    mid = mid.astype(jnp.bfloat16)
    half = mid.shape[0] // 2
    head_ref[...] = mid[:half]
    tail_ref[...] = mid[half:]


def edge_kernel(sizes, nbr_ref, before_ref, head_ref, tail_ref, after_ref, *refs):
    pieces, (out_ref, p_in, p_hid, u_in, u_hid) = refs[:-5], refs[-5:]
    unpack(pieces, sizes, {0: p_in, 1: p_hid, 2: u_in, 3: u_hid})
    rows, fanin = nbr_ref.shape
    width = head_ref.shape[1]
    mid = jnp.concatenate([head_ref[...], tail_ref[...]], axis=0)
    extended = jnp.concatenate([before_ref[...], mid, after_ref[...]], axis=0)
    spots = lax.broadcasted_iota(jnp.int32, (rows, extended.shape[0]), 1)
    nbr = nbr_ref[...]
    receivers = dot(mid, p_in[width:])
    total = None
    group = 2 if fanin % 2 == 0 else 1
    for at in range(0, fanin, group):
        chosen = jnp.concatenate(
            [
                jnp.where(spots == nbr[:, k : k + 1], 1.0, 0.0).astype(jnp.bfloat16)
                for k in range(at, at + group)
            ],
            axis=0,
        )
        senders = dot(chosen, extended).astype(jnp.bfloat16)
        hidden = dot(senders, p_in[:width])
        hidden = (hidden.reshape(group, rows, width) + receivers[None]).reshape(group * rows, width)
        edges = layer_norm(dot(silu(hidden).astype(jnp.bfloat16), p_hid[...]))
        for k in range(group):
            one = edges[k * rows : (k + 1) * rows]
            total = one if total is None else total + one
    hidden = dot(mid, u_in[:width]) + dot(total.astype(jnp.bfloat16), u_in[width:])
    hidden = silu(hidden).astype(jnp.bfloat16)
    out = mid.astype(jnp.float32) + layer_norm(dot(hidden, u_hid[...]))
    out_ref[...] = out.astype(jnp.bfloat16)


def shards(
    grid_lat,
    grid_route,
    grid_slot,
    mesh_lat,
    mesh_nbr,
    enc_w1,
    enc_w2,
    grid_w1,
    grid_w2,
    node_w1,
    node_w2,
    proc_w1,
    proc_w2,
    upd_w1,
    upd_w2,
):
    grid_rows, width = grid_lat.shape
    mesh_rows = mesh_lat.shape[0]
    faces = lax.axis_size("face")
    bands, subs = lax.axis_size("band"), lax.axis_size("sub")
    count = bands * subs
    f32, bf16 = jnp.float32, jnp.bfloat16

    def matrix(weight):
        return pltpu.VMEM((weight.shape[0] * count, weight.shape[1]), bf16)

    def cost(rows, depth):
        return pl.CostEstimate(
            flops=2 * rows * depth * width,
            bytes_accessed=2 * (rows + depth) * width,
            transcendentals=rows * width,
        )

    sets = ((node_w1, node_w2, grid_w1, grid_w2), (proc_w1, proc_w2, upd_w1, upd_w2))
    sizes = [[weight.shape[0] for weight in one] for one in sets]
    enc_far = [[shift(one, "band", step) for step in range(1, bands)] for one in (enc_w1, enc_w2)]
    enc_all = [
        own_spread(one) + relay(far) for one, far in zip((enc_w1, enc_w2), enc_far)
    ]
    early, late = pack(sets)
    early_sent = after(early, *enc_far[1], *enc_all[0][1:], *enc_all[1][1:subs])
    early_far = [shift(early_sent, "band", step) for step in range(1, bands)]
    early_near, late_near = own_spread(early), own_spread(late)

    me = lax.axis_index("face")
    routes = grid_route[:, 0]
    steps = distances(faces)
    distance = lax.rem(routes - me + faces, faces) if faces & (faces - 1) else routes ^ me
    targets = (distance * mesh_rows + grid_slot).reshape(1, grid_rows)

    block = (mesh_rows, width)
    sums = pl.pallas_call(
        functools.partial(encode_kernel, count, faces, mesh_rows),
        out_shape=[
            jax.ShapeDtypeStruct(block, bf16 if step else f32) for step in range(faces)
        ],
        in_specs=[VMEM, VMEM] + [VMEM] * (2 * count),
        out_specs=[VMEM] * faces,
        scratch_shapes=[
            matrix(enc_w1),
            matrix(enc_w2),
            pltpu.VMEM((grid_rows, width), bf16),
        ],
        compiler_params=pltpu.CompilerParams(vmem_limit_bytes=16 * MIB),
        cost_estimate=cost(grid_rows, 3 * width),
        name="encode",
    )(targets, grid_lat, *enc_all[0], *enc_all[1])
    late_sent = after(late, sums[0])
    late_far = [shift(late_sent, "band", step) for step in range(1, bands)]
    arrived = [sums[0]] + [to_face(sums[step], step) for step in steps[1:]]

    early_all = early_near + relay(early_far, *arrived[1:])
    grid_out = pl.pallas_call(
        functools.partial(grid_kernel, sizes[0]),
        out_shape=jax.ShapeDtypeStruct(grid_lat.shape, bf16),
        in_specs=[VMEM] + [VMEM] * len(early_all),
        out_specs=VMEM,
        scratch_shapes=[matrix(grid_w1), matrix(grid_w2)],
        compiler_params=pltpu.CompilerParams(vmem_limit_bytes=16 * MIB),
        cost_estimate=cost(grid_rows, 2 * width),
        name="grid_update",
    )(grid_lat, *early_all)

    half = (mesh_rows // 2, width)
    head, tail = pl.pallas_call(
        functools.partial(node_kernel, sizes[0], faces),
        out_shape=[jax.ShapeDtypeStruct(half, bf16)] * 2,
        in_specs=[VMEM] * (1 + faces) + [VMEM] * len(early_all),
        out_specs=[VMEM] * 2,
        scratch_shapes=[matrix(node_w1), matrix(node_w2)],
        compiler_params=pltpu.CompilerParams(vmem_limit_bytes=16 * MIB),
        cost_estimate=cost(mesh_rows, 3 * width),
        name="node_update",
    )(mesh_lat, *arrived, *early_all)

    before = shift(tail, "face", 1)
    behind = shift(head, "face", faces - 1)
    late_all = late_near + relay(late_far, before, behind, grid_out)
    mesh_out = pl.pallas_call(
        functools.partial(edge_kernel, sizes[1]),
        out_shape=jax.ShapeDtypeStruct(mesh_lat.shape, bf16),
        in_specs=[VMEM] * 5 + [VMEM] * len(late_all),
        out_specs=VMEM,
        scratch_shapes=[
            matrix(proc_w1),
            matrix(proc_w2),
            matrix(upd_w1),
            matrix(upd_w2),
        ],
        compiler_params=pltpu.CompilerParams(vmem_limit_bytes=16 * MIB),
        cost_estimate=cost(mesh_rows * mesh_nbr.shape[1], 3 * width),
        name="edge_update",
    )(mesh_nbr, before, head, tail, behind, *late_all)
    return (grid_out, mesh_out)


def solution(mesh):
    rows = ("groups", "face", "band", "sub")
    placed = (
        P(rows, None),
        P(rows, None),
        P(rows),
        P(rows, None),
        P(rows, None),
    ) + (P(("band", "sub"), None),) * 10
    return jax.shard_map(
        shards,
        mesh=mesh,
        in_specs=placed,
        out_specs=(P(rows, None), P(rows, None)),
        check_vma=False,
    )
```

```python
import functools

import jax
import jax.numpy as jnp
from jax import lax
from jax.experimental import pallas as pl
from jax.experimental.pallas import tpu as pltpu
from jax.sharding import PartitionSpec as P

MIB = 1 << 20
VMEM = pl.BlockSpec(memory_space=pltpu.VMEM)


def after(value, *earlier):
    return lax.optimization_barrier((value, *earlier))[0]


def shift(value, axis, step):
    count = lax.axis_size(axis)
    return lax.ppermute(value, axis, [(i, (i + step) % count) for i in range(count)])


def distances(faces):
    if faces & (faces - 1):
        return list(range(faces))
    return [0] + sorted(range(1, faces), key=lambda step: (step == 1, step))


def face_at(faces, step, me):
    return (me + step) % faces if faces & (faces - 1) else me ^ step


def to_face(value, step):
    faces = lax.axis_size("face")
    return lax.ppermute(value, "face", [(i, face_at(faces, step, i)) for i in range(faces)])


def own_spread(pack):
    return [pack] + [shift(pack, "sub", step) for step in range(1, lax.axis_size("sub"))]


def relay(parts, *earlier):
    pieces = []
    for part in parts:
        pieces.extend(own_spread(after(part, *earlier) if earlier else part))
    return pieces


def owner_of(band_step, sub_step):
    bands, subs = lax.axis_size("band"), lax.axis_size("sub")
    return lax.rem(lax.axis_index("band") + bands - band_step, bands) * subs + lax.rem(
        lax.axis_index("sub") + subs - sub_step, subs
    )


def place(pieces, start, rows, whole):
    subs = lax.axis_size("sub")
    for index, piece in enumerate(pieces):
        owner = owner_of(index // subs, index % subs)
        whole[pl.ds(pl.multiple_of(owner * rows, rows), rows)] = piece[start : start + rows]


def unpack_parts(pieces, base, sizes, wholes):
    subs, groups = lax.axis_size("sub"), lax.axis_size("groups")
    for index, piece in enumerate(pieces):
        band_step, rest = divmod(index, groups * subs)
        owner = owner_of(band_step + 1, rest % subs)
        part = lax.rem(lax.axis_index("groups") + groups - rest // subs, groups)
        start = base if rest < subs else 0
        for size, whole in zip(sizes, wholes):
            rows = size // groups
            into = pl.multiple_of(owner * size + part * rows, rows)
            whole[pl.ds(into, rows)] = piece[start : start + rows]
            start += rows


def unpack(pieces, sizes, wanted):
    for at, whole in wanted.items():
        place(pieces, sum(sizes[:at]), sizes[at], whole)


def pack_kernel(sets, *refs):
    sources, outs = refs[: -len(sets)], refs[-len(sets) :]
    group = lax.axis_index("groups")
    for out, members in zip(outs, sets):
        start = 0
        for member, rows in members:
            source = sources[member]
            if rows < source.shape[0]:
                out[start : start + rows] = source[pl.ds(pl.multiple_of(group * rows, rows), rows)]
            else:
                out[start : start + rows] = source[...]
            start += rows


def pack(weights, sets):
    return pl.pallas_call(
        functools.partial(pack_kernel, sets),
        out_shape=[
            jax.ShapeDtypeStruct(
                (sum(rows for _, rows in members), weights[0].shape[1]), jnp.bfloat16
            )
            for members in sets
        ],
        in_specs=[VMEM] * len(weights),
        out_specs=[VMEM] * len(sets),
        name="pack",
    )(*weights)


def silu(values):
    half = 0.5 * values
    return half + half * jnp.tanh(half)


def layer_norm(values):
    average = jnp.mean(values, axis=-1, keepdims=True)
    centred = values - average
    spread_of = jnp.mean(centred * centred, axis=-1, keepdims=True)
    return centred * lax.rsqrt(spread_of + 1e-05)


def dot(a, b):
    return jnp.dot(a, b, preferred_element_type=jnp.float32)


def encode_kernel(count, faces, mesh_rows, target_ref, lat_ref, *refs):
    in_pieces, hid_pieces = refs[:count], refs[count : 2 * count]
    outs = refs[2 * count : 2 * count + faces]
    w_in, w_hid, messages = refs[2 * count + faces :]
    rows = w_in.shape[0] // count
    place(in_pieces, 0, rows, w_in)
    place(hid_pieces, 0, rows, w_hid)
    block = 256
    for start in range(0, lat_ref.shape[0], block):
        here = pl.ds(start, block)
        hidden = silu(dot(lat_ref[here], w_in[...])).astype(jnp.bfloat16)
        messages[here] = layer_norm(dot(hidden, w_hid[...])).astype(jnp.bfloat16)
    group = min(faces, 4)
    for at in range(0, faces, group):
        slots = lax.broadcasted_iota(jnp.int32, (group * mesh_rows, lat_ref.shape[0]), 0)
        chosen = jnp.where(slots + at * mesh_rows == target_ref[...], 1.0, 0.0)
        chosen = chosen.astype(jnp.bfloat16)
        sums = dot(chosen, messages[...])
        for face in range(group):
            out = outs[at + face]
            out[...] = sums[face * mesh_rows : (face + 1) * mesh_rows].astype(out.dtype)


def grid_kernel(base, sizes, lat_ref, *refs):
    pieces, (out_ref, w_in, w_hid) = refs[:-3], refs[-3:]
    subs = lax.axis_size("sub")
    unpack(pieces[:subs], sizes, {2: w_in, 3: w_hid})
    unpack_parts(pieces[subs:], base, sizes[2:], [w_in, w_hid])
    block = 256
    for start in range(0, lat_ref.shape[0], block):
        here = pl.ds(start, block)
        lat = lat_ref[here]
        hidden = silu(dot(lat, w_in[...])).astype(jnp.bfloat16)
        out = lat.astype(jnp.float32) + layer_norm(dot(hidden, w_hid[...]))
        out_ref[here] = out.astype(jnp.bfloat16)


def node_kernel(sizes, faces, lat_ref, *refs):
    sums, pieces = refs[:faces], refs[faces:-4]
    head_ref, tail_ref, w_in, w_hid = refs[-4:]
    width = lat_ref.shape[1]
    unpack(pieces, sizes, {0: w_in, 1: w_hid})
    collected = sums[0][...]
    for one in sums[1:]:
        collected = collected + one[...].astype(jnp.float32)
    lat = lat_ref[...]
    hidden = dot(lat, w_in[:width]) + dot(collected.astype(jnp.bfloat16), w_in[width:])
    hidden = silu(hidden).astype(jnp.bfloat16)
    mid = lat.astype(jnp.float32) + layer_norm(dot(hidden, w_hid[...]))
    mid = mid.astype(jnp.bfloat16)
    half = mid.shape[0] // 2
    head_ref[...] = mid[:half]
    tail_ref[...] = mid[half:]


def edge_kernel(sizes, nbr_ref, before_ref, head_ref, tail_ref, after_ref, *refs):
    pieces, (out_ref, p_in, p_hid, u_in, u_hid) = refs[:-5], refs[-5:]
    unpack(pieces, sizes, {0: p_in, 1: p_hid, 2: u_in, 3: u_hid})
    rows, fanin = nbr_ref.shape
    width = head_ref.shape[1]
    mid = jnp.concatenate([head_ref[...], tail_ref[...]], axis=0)
    extended = jnp.concatenate([before_ref[...], mid, after_ref[...]], axis=0)
    spots = lax.broadcasted_iota(jnp.int32, (rows, extended.shape[0]), 1)
    nbr = nbr_ref[...]
    receivers = dot(mid, p_in[width:])
    total = None
    group = fanin
    for at in range(0, fanin, group):
        chosen = jnp.concatenate(
            [
                jnp.where(spots == nbr[:, k : k + 1], 1.0, 0.0).astype(jnp.bfloat16)
                for k in range(at, at + group)
            ],
            axis=0,
        )
        senders = dot(chosen, extended).astype(jnp.bfloat16)
        hidden = dot(senders, p_in[:width])
        hidden = (hidden.reshape(group, rows, width) + receivers[None]).reshape(group * rows, width)
        edges = layer_norm(dot(silu(hidden).astype(jnp.bfloat16), p_hid[...]))
        for k in range(group):
            one = edges[k * rows : (k + 1) * rows]
            total = one if total is None else total + one
    hidden = dot(mid, u_in[:width]) + dot(total.astype(jnp.bfloat16), u_in[width:])
    hidden = silu(hidden).astype(jnp.bfloat16)
    out = mid.astype(jnp.float32) + layer_norm(dot(hidden, u_hid[...]))
    out_ref[...] = out.astype(jnp.bfloat16)


def shards(
    grid_lat,
    grid_route,
    grid_slot,
    mesh_lat,
    mesh_nbr,
    enc_w1,
    enc_w2,
    grid_w1,
    grid_w2,
    node_w1,
    node_w2,
    proc_w1,
    proc_w2,
    upd_w1,
    upd_w2,
):
    grid_rows, width = grid_lat.shape
    mesh_rows = mesh_lat.shape[0]
    faces = lax.axis_size("face")
    bands, subs = lax.axis_size("band"), lax.axis_size("sub")
    count = bands * subs
    f32, bf16 = jnp.float32, jnp.bfloat16

    def matrix(weight):
        return pltpu.VMEM((weight.shape[0] * count, weight.shape[1]), bf16)

    def cost(rows, depth):
        return pl.CostEstimate(
            flops=2 * rows * depth * width,
            bytes_accessed=2 * (rows + depth) * width,
            transcendentals=rows * width,
        )

    early_set = (node_w1, node_w2, grid_w1, grid_w2)
    late_set = (proc_w1, proc_w2, upd_w1, upd_w2)
    early_sizes = [weight.shape[0] for weight in early_set]
    late_sizes = [weight.shape[0] for weight in late_set]
    small = pl.CostEstimate(flops=1, bytes_accessed=1, transcendentals=0)
    enc_far = [[shift(one, "band", step) for step in range(1, bands)] for one in (enc_w1, enc_w2)]
    enc_all = [
        own_spread(one) + relay(far) for one, far in zip((enc_w1, enc_w2), enc_far)
    ]
    groups = lax.axis_size("groups")
    early_rows = list(enumerate(early_sizes))
    late_rows = list(enumerate(late_sizes, len(early_sizes)))
    halves = [(at, rows // groups) for at, rows in early_rows[2:]]
    early, late, first = pack(
        early_set + late_set, (early_rows, late_rows, early_rows[:2] + halves)
    )
    first_sent = after(first, *enc_far[0], *enc_far[1])
    first_far = [shift(first_sent, "band", step) for step in range(1, bands)]
    own_enc = enc_all[0][1:subs] + enc_all[1][1:subs]
    early_near = own_spread(after(early, *enc_far[0], *enc_far[1], *own_enc))
    late_near = own_spread(late)

    me = lax.axis_index("face")
    routes = grid_route[:, 0]
    steps = distances(faces)
    distance = lax.rem(routes - me + faces, faces) if faces & (faces - 1) else routes ^ me
    targets = (distance * mesh_rows + grid_slot).reshape(1, grid_rows)

    block = (mesh_rows, width)
    sums = pl.pallas_call(
        functools.partial(encode_kernel, count, faces, mesh_rows),
        out_shape=[
            jax.ShapeDtypeStruct(block, bf16 if step else f32) for step in range(faces)
        ],
        in_specs=[VMEM, VMEM] + [VMEM] * (2 * count),
        out_specs=[VMEM] * faces,
        scratch_shapes=[
            matrix(enc_w1),
            matrix(enc_w2),
            pltpu.VMEM((grid_rows, width), bf16),
        ],
        compiler_params=pltpu.CompilerParams(vmem_limit_bytes=16 * MIB),
        cost_estimate=cost(grid_rows, 3 * width),
        name="encode",
    )(after(targets, *early_near[1:]), grid_lat, *enc_all[0], *enc_all[1])
    late_sent = after(late, sums[0])
    late_far = [shift(late_sent, "band", step) for step in range(1, bands)]
    arrived = [sums[0]] + [to_face(sums[step], step) for step in steps[1:]]

    first_all = relay(first_far, *arrived[1:])
    node_all = early_near + first_all

    half = (mesh_rows // 2, width)
    head, tail = pl.pallas_call(
        functools.partial(node_kernel, early_sizes, faces),
        out_shape=[jax.ShapeDtypeStruct(half, bf16)] * 2,
        in_specs=[VMEM] * (1 + faces) + [VMEM] * len(node_all),
        out_specs=[VMEM] * 2,
        scratch_shapes=[matrix(node_w1), matrix(node_w2)],
        compiler_params=pltpu.CompilerParams(vmem_limit_bytes=16 * MIB),
        cost_estimate=small,
        name="node_update",
    )(mesh_lat, *arrived, *node_all)

    base = sum(early_sizes[:2])
    grid_all = list(early_near)
    for at, one in enumerate(first_far):
        over = after(one[base:], *arrived[1:])
        grid_all += first_all[at * subs : (at + 1) * subs]
        grid_all += relay([shift(over, "groups", step) for step in range(1, groups)], head)
    grid_out = pl.pallas_call(
        functools.partial(grid_kernel, base, early_sizes),
        out_shape=jax.ShapeDtypeStruct(grid_lat.shape, bf16),
        in_specs=[VMEM] + [VMEM] * len(grid_all),
        out_specs=VMEM,
        scratch_shapes=[matrix(grid_w1), matrix(grid_w2)],
        compiler_params=pltpu.CompilerParams(vmem_limit_bytes=16 * MIB),
        cost_estimate=small,
        name="grid_update",
    )(grid_lat, *grid_all)

    before = shift(tail, "face", 1)
    behind = shift(head, "face", faces - 1)
    late_all = late_near + relay(late_far, before, behind, grid_out)
    mesh_out = pl.pallas_call(
        functools.partial(edge_kernel, late_sizes),
        out_shape=jax.ShapeDtypeStruct(mesh_lat.shape, bf16),
        in_specs=[VMEM] * 5 + [VMEM] * len(late_all),
        out_specs=VMEM,
        scratch_shapes=[
            matrix(proc_w1),
            matrix(proc_w2),
            matrix(upd_w1),
            matrix(upd_w2),
        ],
        compiler_params=pltpu.CompilerParams(vmem_limit_bytes=16 * MIB),
        cost_estimate=cost(mesh_rows * mesh_nbr.shape[1], 3 * width),
        name="edge_update",
    )(mesh_nbr, before, head, tail, behind, *late_all)
    return (grid_out, mesh_out)


def solution(mesh):
    rows = ("groups", "face", "band", "sub")
    placed = (
        P(rows, None),
        P(rows, None),
        P(rows),
        P(rows, None),
        P(rows, None),
    ) + (P(("band", "sub"), None),) * 10
    return jax.shard_map(
        shards,
        mesh=mesh,
        in_specs=placed,
        out_specs=(P(rows, None), P(rows, None)),
        check_vma=False,
    )
```

```python
import functools

import jax
import jax.numpy as jnp
from jax import lax
from jax.experimental import pallas as pl
from jax.experimental.pallas import tpu as pltpu
from jax.sharding import PartitionSpec as P

MIB = 1 << 20
VMEM = pl.BlockSpec(memory_space=pltpu.VMEM)


def after(value, *earlier):
    return lax.optimization_barrier((value, *earlier))[0]


def shift(value, axis, step):
    count = lax.axis_size(axis)
    return lax.ppermute(value, axis, [(i, (i + step) % count) for i in range(count)])


def distances(faces):
    if faces & (faces - 1):
        return list(range(faces))
    return [0] + sorted(range(1, faces), key=lambda step: (step == 1, step))


def face_at(faces, step, me):
    return (me + step) % faces if faces & (faces - 1) else me ^ step


def to_face(value, step):
    faces = lax.axis_size("face")
    return lax.ppermute(value, "face", [(i, face_at(faces, step, i)) for i in range(faces)])


def own_spread(pack):
    return [pack] + [shift(pack, "sub", step) for step in range(1, lax.axis_size("sub"))]


def relay(parts, *earlier):
    pieces = []
    for part in parts:
        pieces.extend(own_spread(after(part, *earlier) if earlier else part))
    return pieces


def owner_of(band_step, sub_step):
    bands, subs = lax.axis_size("band"), lax.axis_size("sub")
    return lax.rem(lax.axis_index("band") + bands - band_step, bands) * subs + lax.rem(
        lax.axis_index("sub") + subs - sub_step, subs
    )


def place(near, far, near_start, far_start, rows, whole):
    subs = lax.axis_size("sub")
    for index, piece in enumerate([*near, *far]):
        owner = owner_of(index // subs, index % subs)
        start = near_start if index < subs else far_start
        whole[pl.ds(pl.multiple_of(owner * rows, rows), rows)] = piece[start : start + rows]


def unpack(pieces, near_start, far_start, wholes):
    subs, count = lax.axis_size("sub"), len(pieces)
    for whole in wholes:
        rows = whole.shape[0] // count
        place(pieces[:subs], pieces[subs:], near_start, far_start, rows, whole)
        near_start, far_start = near_start + rows, far_start + rows


def unpack_parts(pieces, start, wholes):
    subs, groups = lax.axis_size("sub"), lax.axis_size("groups")
    count = lax.axis_size("band") * subs
    for index, piece in enumerate(pieces):
        band_step, rest = divmod(index, groups * subs)
        owner = owner_of(band_step + 1, rest % subs)
        part = lax.rem(lax.axis_index("groups") + groups - rest // subs, groups)
        begin = start if rest < subs else 0
        for whole in wholes:
            rows = whole.shape[0] // (count * groups)
            into = pl.multiple_of((owner * groups + part) * rows, rows)
            whole[pl.ds(into, rows)] = piece[begin : begin + rows]
            begin += rows


def pack_kernel(sets, *refs):
    sources, outs = refs[: -len(sets)], refs[-len(sets) :]
    group = lax.axis_index("groups")
    for out, members in zip(outs, sets):
        start = 0
        for member, rows in members:
            source = sources[member]
            if rows < source.shape[0]:
                out[start : start + rows] = source[pl.ds(pl.multiple_of(group * rows, rows), rows)]
            else:
                out[start : start + rows] = source[...]
            start += rows


def pack(weights, sets):
    return pl.pallas_call(
        functools.partial(pack_kernel, sets),
        out_shape=[
            jax.ShapeDtypeStruct(
                (sum(rows for _, rows in members), weights[0].shape[1]), jnp.bfloat16
            )
            for members in sets
        ],
        in_specs=[VMEM] * len(weights),
        out_specs=[VMEM] * len(sets),
        name="pack",
    )(*weights)


def silu(values):
    half = 0.5 * values
    return half + half * jnp.tanh(half)


def layer_norm(values):
    average = jnp.mean(values, axis=-1, keepdims=True)
    centred = values - average
    spread_of = jnp.mean(centred * centred, axis=-1, keepdims=True)
    return centred * lax.rsqrt(spread_of + 1e-05)


def dot(a, b):
    return jnp.dot(a, b, preferred_element_type=jnp.float32)


def encode_kernel(count, faces, mesh_rows, target_ref, lat_ref, *refs):
    in_pieces, hid_pieces = refs[:count], refs[count : 2 * count]
    outs = refs[2 * count : 2 * count + faces]
    w_in, w_hid, messages = refs[2 * count + faces :]
    unpack(in_pieces, 0, 0, [w_in])
    unpack(hid_pieces, 0, 0, [w_hid])
    block = 256
    for start in range(0, lat_ref.shape[0], block):
        here = pl.ds(start, block)
        hidden = silu(dot(lat_ref[here], w_in[...])).astype(jnp.bfloat16)
        messages[here] = layer_norm(dot(hidden, w_hid[...])).astype(jnp.bfloat16)
    group = min(faces, 4)
    for at in range(0, faces, group):
        slots = lax.broadcasted_iota(jnp.int32, (group * mesh_rows, lat_ref.shape[0]), 0)
        chosen = jnp.where(slots + at * mesh_rows == target_ref[...], 1.0, 0.0)
        chosen = chosen.astype(jnp.bfloat16)
        sums = dot(chosen, messages[...])
        for face in range(group):
            out = outs[at + face]
            out[...] = sums[face * mesh_rows : (face + 1) * mesh_rows].astype(out.dtype)


def grid_kernel(near_start, part_start, lat_ref, *refs):
    pieces, (out_ref, w_in, w_hid) = refs[:-3], refs[-3:]
    subs = lax.axis_size("sub")
    start = near_start
    for whole in (w_in, w_hid):
        rows = whole.shape[0] // (lax.axis_size("band") * subs)
        place(pieces[:subs], [], start, 0, rows, whole)
        start += rows
    unpack_parts(pieces[subs:], part_start, [w_in, w_hid])
    block = 256
    for start in range(0, lat_ref.shape[0], block):
        here = pl.ds(start, block)
        lat = lat_ref[here]
        hidden = silu(dot(lat, w_in[...])).astype(jnp.bfloat16)
        out = lat.astype(jnp.float32) + layer_norm(dot(hidden, w_hid[...]))
        out_ref[here] = out.astype(jnp.bfloat16)


def node_kernel(faces, lat_ref, *refs):
    sums, pieces = refs[:faces], refs[faces:-4]
    head_ref, tail_ref, w_in, w_hid = refs[-4:]
    width = lat_ref.shape[1]
    unpack(pieces, 0, 0, [w_in, w_hid])
    collected = sums[0][...]
    for one in sums[1:]:
        collected = collected + one[...].astype(jnp.float32)
    lat = lat_ref[...]
    hidden = dot(lat, w_in[:width]) + dot(collected.astype(jnp.bfloat16), w_in[width:])
    hidden = silu(hidden).astype(jnp.bfloat16)
    mid = lat.astype(jnp.float32) + layer_norm(dot(hidden, w_hid[...]))
    mid = mid.astype(jnp.bfloat16)
    half = mid.shape[0] // 2
    head_ref[...] = mid[:half]
    tail_ref[...] = mid[half:]


def edge_kernel(far_start, nbr_ref, before_ref, head_ref, tail_ref, after_ref, *refs):
    pieces, (out_ref, p_in, p_hid) = refs[:-3], refs[-3:]
    unpack(pieces, 0, far_start, [p_in, p_hid])
    rows, fanin = nbr_ref.shape
    width = head_ref.shape[1]
    mid = jnp.concatenate([head_ref[...], tail_ref[...]], axis=0)
    extended = jnp.concatenate([before_ref[...], mid, after_ref[...]], axis=0)
    spots = lax.broadcasted_iota(jnp.int32, (rows, extended.shape[0]), 1)
    nbr = nbr_ref[...]
    receivers = dot(mid, p_in[width:])
    total = None
    group = fanin
    for at in range(0, fanin, group):
        chosen = jnp.concatenate(
            [
                jnp.where(spots == nbr[:, k : k + 1], 1.0, 0.0).astype(jnp.bfloat16)
                for k in range(at, at + group)
            ],
            axis=0,
        )
        senders = dot(chosen, extended).astype(jnp.bfloat16)
        hidden = dot(senders, p_in[:width])
        hidden = (hidden.reshape(group, rows, width) + receivers[None]).reshape(group * rows, width)
        edges = layer_norm(dot(silu(hidden).astype(jnp.bfloat16), p_hid[...]))
        for k in range(group):
            one = edges[k * rows : (k + 1) * rows]
            total = one if total is None else total + one
    out_ref[...] = total.astype(jnp.bfloat16)


def update_kernel(near_start, head_ref, tail_ref, sum_ref, *refs):
    pieces, (out_ref, w_in, w_hid) = refs[:-3], refs[-3:]
    unpack(pieces, near_start, 0, [w_in, w_hid])
    width = head_ref.shape[1]
    mid = jnp.concatenate([head_ref[...], tail_ref[...]], axis=0)
    hidden = dot(mid, w_in[:width]) + dot(sum_ref[...], w_in[width:])
    hidden = silu(hidden).astype(jnp.bfloat16)
    out = mid.astype(jnp.float32) + layer_norm(dot(hidden, w_hid[...]))
    out_ref[...] = out.astype(jnp.bfloat16)


def shards(
    grid_lat,
    grid_route,
    grid_slot,
    mesh_lat,
    mesh_nbr,
    enc_w1,
    enc_w2,
    grid_w1,
    grid_w2,
    node_w1,
    node_w2,
    proc_w1,
    proc_w2,
    upd_w1,
    upd_w2,
):
    grid_rows, width = grid_lat.shape
    mesh_rows = mesh_lat.shape[0]
    faces = lax.axis_size("face")
    bands, subs = lax.axis_size("band"), lax.axis_size("sub")
    count = bands * subs
    f32, bf16 = jnp.float32, jnp.bfloat16

    def matrix(weight):
        return pltpu.VMEM((weight.shape[0] * count, weight.shape[1]), bf16)

    def cost(rows, depth):
        return pl.CostEstimate(
            flops=2 * rows * depth * width,
            bytes_accessed=2 * (rows + depth) * width,
            transcendentals=rows * width,
        )

    small = pl.CostEstimate(flops=1, bytes_accessed=1, transcendentals=0)
    enc_far = [[shift(one, "band", step) for step in range(1, bands)] for one in (enc_w1, enc_w2)]
    enc_all = [
        own_spread(one) + relay(far) for one, far in zip((enc_w1, enc_w2), enc_far)
    ]
    groups = lax.axis_size("groups")
    weights = (node_w1, node_w2, grid_w1, grid_w2, proc_w1, proc_w2, upd_w1, upd_w2)
    whole = [(at, weight.shape[0]) for at, weight in enumerate(weights)]
    halves = [(at, rows // groups) for at, rows in whole[2:4]]
    node_rows = node_w1.shape[0] + node_w2.shape[0]
    proc_rows = proc_w1.shape[0] + proc_w2.shape[0]
    early, late, first, last = pack(
        weights, (whole[:4], whole[4:], whole[:2] + whole[4:6] + halves, whole[6:])
    )
    own_enc = enc_all[0][1:subs] + enc_all[1][1:subs]
    first_sent = after(first, *enc_far[0], *enc_far[1], *own_enc)
    first_far = [shift(first_sent, "band", step) for step in range(1, bands)]
    early_near = own_spread(early)

    me = lax.axis_index("face")
    routes = grid_route[:, 0]
    steps = distances(faces)
    distance = lax.rem(routes - me + faces, faces) if faces & (faces - 1) else routes ^ me
    targets = (distance * mesh_rows + grid_slot).reshape(1, grid_rows)

    block = (mesh_rows, width)
    sums = pl.pallas_call(
        functools.partial(encode_kernel, count, faces, mesh_rows),
        out_shape=[
            jax.ShapeDtypeStruct(block, bf16 if step else f32) for step in range(faces)
        ],
        in_specs=[VMEM, VMEM] + [VMEM] * (2 * count),
        out_specs=[VMEM] * faces,
        scratch_shapes=[
            matrix(enc_w1),
            matrix(enc_w2),
            pltpu.VMEM((grid_rows, width), bf16),
        ],
        compiler_params=pltpu.CompilerParams(vmem_limit_bytes=16 * MIB),
        cost_estimate=cost(grid_rows, 3 * width),
        name="encode",
    )(targets, grid_lat, *enc_all[0], *enc_all[1])
    last_sent = after(last, sums[0])
    last_far = [shift(last_sent, "band", step) for step in range(1, bands)]
    arrived = [sums[0]] + [to_face(sums[step], step) for step in steps[1:]]
    first_all = relay(first_far, *arrived[1:], *early_near[1:])

    half = (mesh_rows // 2, width)
    head, tail = pl.pallas_call(
        functools.partial(node_kernel, faces),
        out_shape=[jax.ShapeDtypeStruct(half, bf16)] * 2,
        in_specs=[VMEM] * (1 + faces) + [VMEM] * count,
        out_specs=[VMEM] * 2,
        scratch_shapes=[matrix(node_w1), matrix(node_w2)],
        compiler_params=pltpu.CompilerParams(vmem_limit_bytes=16 * MIB),
        cost_estimate=small,
        name="node_update",
    )(mesh_lat, *arrived, *early_near, *first_all)

    parts, crossed = [], []
    for at, one in enumerate(first_far):
        over = after(one[node_rows + proc_rows :], *arrived[1:])
        others = [shift(over, "groups", step) for step in range(1, groups)]
        parts += first_all[at * subs : (at + 1) * subs] + relay(others, head)
        crossed += others
    before = shift(after(tail, *crossed), "face", 1)
    behind = shift(after(head, *crossed), "face", faces - 1)
    grid_out = pl.pallas_call(
        functools.partial(grid_kernel, node_rows, node_rows + proc_rows),
        out_shape=jax.ShapeDtypeStruct(grid_lat.shape, bf16),
        in_specs=[VMEM] * (1 + subs + len(parts)),
        out_specs=VMEM,
        scratch_shapes=[matrix(grid_w1), matrix(grid_w2)],
        compiler_params=pltpu.CompilerParams(vmem_limit_bytes=16 * MIB),
        cost_estimate=small,
        name="grid_update",
    )(grid_lat, *early_near, *parts)

    late_near = own_spread(after(late, sums[0]))
    edge_sum = pl.pallas_call(
        functools.partial(edge_kernel, node_rows),
        out_shape=jax.ShapeDtypeStruct(mesh_lat.shape, bf16),
        in_specs=[VMEM] * 5 + [VMEM] * count,
        out_specs=VMEM,
        scratch_shapes=[matrix(proc_w1), matrix(proc_w2)],
        compiler_params=pltpu.CompilerParams(vmem_limit_bytes=16 * MIB),
        cost_estimate=small,
        name="edges",
    )(mesh_nbr, before, head, tail, behind, *late_near, *first_all)

    last_all = late_near + relay(last_far, edge_sum)
    mesh_out = pl.pallas_call(
        functools.partial(update_kernel, proc_rows),
        out_shape=jax.ShapeDtypeStruct(mesh_lat.shape, bf16),
        in_specs=[VMEM] * 3 + [VMEM] * count,
        out_specs=VMEM,
        scratch_shapes=[matrix(upd_w1), matrix(upd_w2)],
        compiler_params=pltpu.CompilerParams(vmem_limit_bytes=16 * MIB),
        cost_estimate=small,
        name="update",
    )(head, tail, edge_sum, *last_all)
    return (grid_out, mesh_out)


def solution(mesh):
    rows = ("groups", "face", "band", "sub")
    placed = (
        P(rows, None),
        P(rows, None),
        P(rows),
        P(rows, None),
        P(rows, None),
    ) + (P(("band", "sub"), None),) * 10
    return jax.shard_map(
        shards,
        mesh=mesh,
        in_specs=placed,
        out_specs=(P(rows, None), P(rows, None)),
        check_vma=False,
    )
```

```python
import functools

import jax
import jax.numpy as jnp
from jax import lax
from jax.experimental import pallas as pl
from jax.experimental.pallas import tpu as pltpu
from jax.sharding import PartitionSpec as P

MIB = 1 << 20
VMEM = pl.BlockSpec(memory_space=pltpu.VMEM)


def after(value, *earlier):
    return lax.optimization_barrier((value, *earlier))[0]


def shift(value, axis, step):
    count = lax.axis_size(axis)
    return lax.ppermute(value, axis, [(i, (i + step) % count) for i in range(count)])


def distances(faces):
    if faces & (faces - 1):
        return list(range(faces))
    return [0] + sorted(range(1, faces), key=lambda step: (step == 1, step))


def face_at(faces, step, me):
    return (me + step) % faces if faces & (faces - 1) else me ^ step


def to_face(value, step):
    faces = lax.axis_size("face")
    return lax.ppermute(value, "face", [(i, face_at(faces, step, i)) for i in range(faces)])


def own_spread(pack):
    return [pack] + [shift(pack, "sub", step) for step in range(1, lax.axis_size("sub"))]


def relay(parts, *earlier):
    pieces = []
    for part in parts:
        pieces.extend(own_spread(after(part, *earlier) if earlier else part))
    return pieces


def owner_of(band_step, sub_step):
    bands, subs = lax.axis_size("band"), lax.axis_size("sub")
    return lax.rem(lax.axis_index("band") + bands - band_step, bands) * subs + lax.rem(
        lax.axis_index("sub") + subs - sub_step, subs
    )


def place(pieces, start, rows, whole):
    subs = lax.axis_size("sub")
    for index, piece in enumerate(pieces):
        owner = owner_of(index // subs, index % subs)
        whole[pl.ds(pl.multiple_of(owner * rows, rows), rows)] = piece[start : start + rows]


def unpack(pieces, sizes, wanted):
    for at, whole in wanted.items():
        place(pieces, sum(sizes[:at]), sizes[at], whole)


def pack_kernel(sets, *refs):
    sources, outs = list(refs[: sum(sets)]), refs[sum(sets) :]
    for out, amount in zip(outs, sets):
        start = 0
        for _ in range(amount):
            source = sources.pop(0)
            out[start : start + source.shape[0]] = source[...]
            start += source.shape[0]


def pack(sets):
    width = sets[0][0].shape[1]
    return pl.pallas_call(
        functools.partial(pack_kernel, [len(one) for one in sets]),
        out_shape=[
            jax.ShapeDtypeStruct((sum(weight.shape[0] for weight in one), width), jnp.bfloat16)
            for one in sets
        ],
        in_specs=[VMEM] * sum(len(one) for one in sets),
        out_specs=[VMEM] * len(sets),
        name="pack",
    )(*(weight for one in sets for weight in one))


def silu(values):
    half = 0.5 * values
    return half + half * jnp.tanh(half)


def layer_norm(values):
    average = jnp.mean(values, axis=-1, keepdims=True)
    centred = values - average
    spread_of = jnp.mean(centred * centred, axis=-1, keepdims=True)
    return centred * lax.rsqrt(spread_of + 1e-05)


def dot(a, b):
    return jnp.dot(a, b, preferred_element_type=jnp.float32)


def encode_kernel(count, faces, mesh_rows, target_ref, lat_ref, *refs):
    in_pieces, hid_pieces = refs[:count], refs[count : 2 * count]
    outs = refs[2 * count : 2 * count + faces]
    w_in, w_hid, messages = refs[2 * count + faces :]
    rows = w_in.shape[0] // count
    place(in_pieces, 0, rows, w_in)
    place(hid_pieces, 0, rows, w_hid)
    block = 256
    for start in range(0, lat_ref.shape[0], block):
        here = pl.ds(start, block)
        hidden = silu(dot(lat_ref[here], w_in[...])).astype(jnp.bfloat16)
        messages[here] = layer_norm(dot(hidden, w_hid[...])).astype(jnp.bfloat16)
    group = min(faces, 4)
    for at in range(0, faces, group):
        slots = lax.broadcasted_iota(jnp.int32, (group * mesh_rows, lat_ref.shape[0]), 0)
        chosen = jnp.where(slots + at * mesh_rows == target_ref[...], 1.0, 0.0)
        chosen = chosen.astype(jnp.bfloat16)
        sums = dot(chosen, messages[...])
        for face in range(group):
            out = outs[at + face]
            out[...] = sums[face * mesh_rows : (face + 1) * mesh_rows].astype(out.dtype)


def grid_kernel(sizes, lat_ref, *refs):
    pieces, (out_ref, w_in, w_hid) = refs[:-3], refs[-3:]
    unpack(pieces, sizes, {2: w_in, 3: w_hid})
    block = 256
    for start in range(0, lat_ref.shape[0], block):
        here = pl.ds(start, block)
        lat = lat_ref[here]
        hidden = silu(dot(lat, w_in[...])).astype(jnp.bfloat16)
        out = lat.astype(jnp.float32) + layer_norm(dot(hidden, w_hid[...]))
        out_ref[here] = out.astype(jnp.bfloat16)


def node_kernel(sizes, faces, lat_ref, *refs):
    sums, pieces = refs[:faces], refs[faces:-4]
    head_ref, tail_ref, w_in, w_hid = refs[-4:]
    width = lat_ref.shape[1]
    unpack(pieces, sizes, {0: w_in, 1: w_hid})
    collected = sums[0][...]
    for one in sums[1:]:
        collected = collected + one[...].astype(jnp.float32)
    lat = lat_ref[...]
    hidden = dot(lat, w_in[:width]) + dot(collected.astype(jnp.bfloat16), w_in[width:])
    hidden = silu(hidden).astype(jnp.bfloat16)
    mid = lat.astype(jnp.float32) + layer_norm(dot(hidden, w_hid[...]))
    mid = mid.astype(jnp.bfloat16)
    half = mid.shape[0] // 2
    head_ref[...] = mid[:half]
    tail_ref[...] = mid[half:]


def edge_kernel(sizes, nbr_ref, before_ref, head_ref, tail_ref, after_ref, *refs):
    pieces, (out_ref, p_in, p_hid, u_in, u_hid) = refs[:-5], refs[-5:]
    unpack(pieces, sizes, {0: p_in, 1: p_hid, 2: u_in, 3: u_hid})
    rows, fanin = nbr_ref.shape
    width = head_ref.shape[1]
    mid = jnp.concatenate([head_ref[...], tail_ref[...]], axis=0)
    extended = jnp.concatenate([before_ref[...], mid, after_ref[...]], axis=0)
    spots = lax.broadcasted_iota(jnp.int32, (rows, extended.shape[0]), 1)
    nbr = nbr_ref[...]
    receivers = dot(mid, p_in[width:])
    total = None
    group = fanin
    for at in range(0, fanin, group):
        chosen = jnp.concatenate(
            [
                jnp.where(spots == nbr[:, k : k + 1], 1.0, 0.0).astype(jnp.bfloat16)
                for k in range(at, at + group)
            ],
            axis=0,
        )
        senders = dot(chosen, extended).astype(jnp.bfloat16)
        hidden = dot(senders, p_in[:width])
        hidden = (hidden.reshape(group, rows, width) + receivers[None]).reshape(group * rows, width)
        edges = layer_norm(dot(silu(hidden).astype(jnp.bfloat16), p_hid[...]))
        for k in range(group):
            one = edges[k * rows : (k + 1) * rows]
            total = one if total is None else total + one
    hidden = dot(mid, u_in[:width]) + dot(total.astype(jnp.bfloat16), u_in[width:])
    hidden = silu(hidden).astype(jnp.bfloat16)
    out = mid.astype(jnp.float32) + layer_norm(dot(hidden, u_hid[...]))
    out_ref[...] = out.astype(jnp.bfloat16)


def shards(
    grid_lat,
    grid_route,
    grid_slot,
    mesh_lat,
    mesh_nbr,
    enc_w1,
    enc_w2,
    grid_w1,
    grid_w2,
    node_w1,
    node_w2,
    proc_w1,
    proc_w2,
    upd_w1,
    upd_w2,
):
    grid_rows, width = grid_lat.shape
    mesh_rows = mesh_lat.shape[0]
    faces = lax.axis_size("face")
    bands, subs = lax.axis_size("band"), lax.axis_size("sub")
    count = bands * subs
    f32, bf16 = jnp.float32, jnp.bfloat16

    def matrix(weight):
        return pltpu.VMEM((weight.shape[0] * count, weight.shape[1]), bf16)

    def cost(rows, depth):
        return pl.CostEstimate(
            flops=2 * rows * depth * width,
            bytes_accessed=2 * (rows + depth) * width,
            transcendentals=rows * width,
        )

    sets = ((node_w1, node_w2, grid_w1, grid_w2), (proc_w1, proc_w2, upd_w1, upd_w2))
    sizes = [[weight.shape[0] for weight in one] for one in sets]
    enc_far = [[shift(one, "band", step) for step in range(1, bands)] for one in (enc_w1, enc_w2)]
    enc_all = [
        own_spread(one) + relay(far) for one, far in zip((enc_w1, enc_w2), enc_far)
    ]
    early, late = pack(sets)
    early_sent = after(early, *enc_far[0], *enc_far[1], *enc_all[0][1:subs], *enc_all[1][1:subs])
    early_far = [shift(early_sent, "band", step) for step in range(1, bands)]
    early_near, late_near = own_spread(early), own_spread(late)

    me = lax.axis_index("face")
    routes = grid_route[:, 0]
    steps = distances(faces)
    distance = lax.rem(routes - me + faces, faces) if faces & (faces - 1) else routes ^ me
    targets = (distance * mesh_rows + grid_slot).reshape(1, grid_rows)

    block = (mesh_rows, width)
    sums = pl.pallas_call(
        functools.partial(encode_kernel, count, faces, mesh_rows),
        out_shape=[
            jax.ShapeDtypeStruct(block, bf16 if step else f32) for step in range(faces)
        ],
        in_specs=[VMEM, VMEM] + [VMEM] * (2 * count),
        out_specs=[VMEM] * faces,
        scratch_shapes=[
            matrix(enc_w1),
            matrix(enc_w2),
            pltpu.VMEM((grid_rows, width), bf16),
        ],
        compiler_params=pltpu.CompilerParams(vmem_limit_bytes=16 * MIB),
        cost_estimate=cost(grid_rows, 3 * width),
        name="encode",
    )(targets, grid_lat, *enc_all[0], *enc_all[1])
    late_sent = after(late, sums[0])
    late_far = [shift(late_sent, "band", step) for step in range(1, bands)]
    arrived = [sums[0]] + [to_face(sums[step], step) for step in steps[1:]]

    early_all = early_near + relay(early_far, *arrived[1:])
    grid_out = pl.pallas_call(
        functools.partial(grid_kernel, sizes[0]),
        out_shape=jax.ShapeDtypeStruct(grid_lat.shape, bf16),
        in_specs=[VMEM] + [VMEM] * len(early_all),
        out_specs=VMEM,
        scratch_shapes=[matrix(grid_w1), matrix(grid_w2)],
        compiler_params=pltpu.CompilerParams(vmem_limit_bytes=16 * MIB),
        cost_estimate=cost(grid_rows, 2 * width),
        name="grid_update",
    )(grid_lat, *early_all)

    half = (mesh_rows // 2, width)
    head, tail = pl.pallas_call(
        functools.partial(node_kernel, sizes[0], faces),
        out_shape=[jax.ShapeDtypeStruct(half, bf16)] * 2,
        in_specs=[VMEM] * (1 + faces) + [VMEM] * len(early_all),
        out_specs=[VMEM] * 2,
        scratch_shapes=[matrix(node_w1), matrix(node_w2)],
        compiler_params=pltpu.CompilerParams(vmem_limit_bytes=16 * MIB),
        cost_estimate=cost(mesh_rows, 3 * width),
        name="node_update",
    )(mesh_lat, *arrived, *early_all)

    before = shift(tail, "face", 1)
    behind = shift(head, "face", faces - 1)
    late_all = late_near + relay(late_far, before, behind, grid_out)
    mesh_out = pl.pallas_call(
        functools.partial(edge_kernel, sizes[1]),
        out_shape=jax.ShapeDtypeStruct(mesh_lat.shape, bf16),
        in_specs=[VMEM] * 5 + [VMEM] * len(late_all),
        out_specs=VMEM,
        scratch_shapes=[
            matrix(proc_w1),
            matrix(proc_w2),
            matrix(upd_w1),
            matrix(upd_w2),
        ],
        compiler_params=pltpu.CompilerParams(vmem_limit_bytes=16 * MIB),
        cost_estimate=cost(mesh_rows * mesh_nbr.shape[1], 3 * width),
        name="edge_update",
    )(mesh_nbr, before, head, tail, behind, *late_all)
    return (grid_out, mesh_out)


def solution(mesh):
    rows = ("groups", "face", "band", "sub")
    placed = (
        P(rows, None),
        P(rows, None),
        P(rows),
        P(rows, None),
        P(rows, None),
    ) + (P(("band", "sub"), None),) * 10
    return jax.shard_map(
        shards,
        mesh=mesh,
        in_specs=placed,
        out_specs=(P(rows, None), P(rows, None)),
        check_vma=False,
    )
```

```python
import functools

import jax
import jax.numpy as jnp
from jax import lax
from jax.experimental import pallas as pl
from jax.experimental.pallas import tpu as pltpu
from jax.sharding import PartitionSpec as P

MIB = 1 << 20
VMEM = pl.BlockSpec(memory_space=pltpu.VMEM)


def after(value, *earlier):
    return lax.optimization_barrier((value, *earlier))[0]


def shift(value, axis, step):
    count = lax.axis_size(axis)
    return lax.ppermute(value, axis, [(i, (i + step) % count) for i in range(count)])


def distances(faces):
    if faces & (faces - 1):
        return list(range(faces))
    return [0] + sorted(range(1, faces), key=lambda step: (step == 1, step))


def face_at(faces, step, me):
    return (me + step) % faces if faces & (faces - 1) else me ^ step


def to_face(value, step):
    faces = lax.axis_size("face")
    return lax.ppermute(value, "face", [(i, face_at(faces, step, i)) for i in range(faces)])


def own_spread(pack):
    return [pack] + [shift(pack, "sub", step) for step in range(1, lax.axis_size("sub"))]


def relay(parts, *earlier):
    pieces = []
    for part in parts:
        pieces.extend(own_spread(after(part, *earlier) if earlier else part))
    return pieces


def owner_of(band_step, sub_step):
    bands, subs = lax.axis_size("band"), lax.axis_size("sub")
    return lax.rem(lax.axis_index("band") + bands - band_step, bands) * subs + lax.rem(
        lax.axis_index("sub") + subs - sub_step, subs
    )


def unpack(pieces, sizes, wanted):
    subs = lax.axis_size("sub")
    for index, piece in enumerate(pieces):
        owner = owner_of(index // subs, index % subs)
        for at, whole in wanted.items():
            rows, start = sizes[at], sum(sizes[:at])
            whole[pl.ds(pl.multiple_of(owner * rows, rows), rows)] = piece[start : start + rows]


def unpack_parts(pieces, wholes):
    subs, groups = lax.axis_size("sub"), lax.axis_size("groups")
    count = lax.axis_size("band") * subs
    for index, piece in enumerate(pieces):
        band_step, rest = divmod(index, groups * subs)
        owner = owner_of(band_step + 1, rest % subs)
        part = lax.rem(lax.axis_index("groups") + groups - rest // subs, groups)
        begin = 0
        for whole in wholes:
            rows = whole.shape[0] // (count * groups)
            into = pl.multiple_of((owner * groups + part) * rows, rows)
            whole[pl.ds(into, rows)] = piece[begin : begin + rows]
            begin += rows


def pack_kernel(sets, *refs):
    sources, outs = refs[: -len(sets)], refs[-len(sets) :]
    group = lax.axis_index("groups")
    for out, members in zip(outs, sets):
        start = 0
        for member, rows in members:
            source = sources[member]
            if rows < source.shape[0]:
                out[start : start + rows] = source[pl.ds(pl.multiple_of(group * rows, rows), rows)]
            else:
                out[start : start + rows] = source[...]
            start += rows


def pack(weights, sets):
    return pl.pallas_call(
        functools.partial(pack_kernel, sets),
        out_shape=[
            jax.ShapeDtypeStruct(
                (sum(rows for _, rows in members), weights[0].shape[1]), jnp.bfloat16
            )
            for members in sets
        ],
        in_specs=[VMEM] * len(weights),
        out_specs=[VMEM] * len(sets),
        name="pack",
    )(*weights)


def silu(values):
    half = 0.5 * values
    return half + half * jnp.tanh(half)


def layer_norm(values):
    average = jnp.mean(values, axis=-1, keepdims=True)
    centred = values - average
    spread_of = jnp.mean(centred * centred, axis=-1, keepdims=True)
    return centred * lax.rsqrt(spread_of + 1e-05)


def dot(a, b):
    return jnp.dot(a, b, preferred_element_type=jnp.float32)


def encode_kernel(count, faces, mesh_rows, target_ref, lat_ref, *refs):
    in_pieces, hid_pieces = refs[:count], refs[count : 2 * count]
    outs = refs[2 * count : 2 * count + faces]
    w_in, w_hid, messages = refs[2 * count + faces :]
    rows = w_in.shape[0] // count
    unpack(in_pieces, [rows], {0: w_in})
    unpack(hid_pieces, [rows], {0: w_hid})
    block = 256
    for start in range(0, lat_ref.shape[0], block):
        here = pl.ds(start, block)
        hidden = silu(dot(lat_ref[here], w_in[...])).astype(jnp.bfloat16)
        messages[here] = layer_norm(dot(hidden, w_hid[...])).astype(jnp.bfloat16)
    group = min(faces, 4)
    for at in range(0, faces, group):
        slots = lax.broadcasted_iota(jnp.int32, (group * mesh_rows, lat_ref.shape[0]), 0)
        chosen = jnp.where(slots + at * mesh_rows == target_ref[...], 1.0, 0.0)
        chosen = chosen.astype(jnp.bfloat16)
        sums = dot(chosen, messages[...])
        for face in range(group):
            out = outs[at + face]
            out[...] = sums[face * mesh_rows : (face + 1) * mesh_rows].astype(out.dtype)


def grid_kernel(sizes, lat_ref, *refs):
    pieces, (out_ref, w_in, w_hid) = refs[:-3], refs[-3:]
    unpack(pieces, sizes, {2: w_in, 3: w_hid})
    block = 256
    for start in range(0, lat_ref.shape[0], block):
        here = pl.ds(start, block)
        lat = lat_ref[here]
        hidden = silu(dot(lat, w_in[...])).astype(jnp.bfloat16)
        out = lat.astype(jnp.float32) + layer_norm(dot(hidden, w_hid[...]))
        out_ref[here] = out.astype(jnp.bfloat16)


def node_kernel(sizes, faces, lat_ref, *refs):
    sums, pieces = refs[:faces], refs[faces:-4]
    head_ref, tail_ref, w_in, w_hid = refs[-4:]
    width = lat_ref.shape[1]
    unpack(pieces, sizes, {0: w_in, 1: w_hid})
    collected = sums[0][...]
    for one in sums[1:]:
        collected = collected + one[...].astype(jnp.float32)
    lat = lat_ref[...]
    hidden = dot(lat, w_in[:width]) + dot(collected.astype(jnp.bfloat16), w_in[width:])
    hidden = silu(hidden).astype(jnp.bfloat16)
    mid = lat.astype(jnp.float32) + layer_norm(dot(hidden, w_hid[...]))
    mid = mid.astype(jnp.bfloat16)
    half = mid.shape[0] // 2
    head_ref[...] = mid[:half]
    tail_ref[...] = mid[half:]


def edge_kernel(sizes, nbr_ref, before_ref, head_ref, tail_ref, after_ref, *refs):
    pieces, wholes = refs[:-5], refs[-4:]
    out_ref, (p_in, p_hid, u_in, u_hid) = refs[-5], wholes
    subs = lax.axis_size("sub")
    unpack(pieces[:subs], sizes, dict(enumerate(wholes)))
    unpack_parts(pieces[subs:], wholes)
    rows, fanin = nbr_ref.shape
    width = head_ref.shape[1]
    mid = jnp.concatenate([head_ref[...], tail_ref[...]], axis=0)
    extended = jnp.concatenate([before_ref[...], mid, after_ref[...]], axis=0)
    spots = lax.broadcasted_iota(jnp.int32, (rows, extended.shape[0]), 1)
    nbr = nbr_ref[...]
    receivers = dot(mid, p_in[width:])
    total = None
    group = fanin
    for at in range(0, fanin, group):
        chosen = jnp.concatenate(
            [
                jnp.where(spots == nbr[:, k : k + 1], 1.0, 0.0).astype(jnp.bfloat16)
                for k in range(at, at + group)
            ],
            axis=0,
        )
        senders = dot(chosen, extended).astype(jnp.bfloat16)
        hidden = dot(senders, p_in[:width])
        hidden = (hidden.reshape(group, rows, width) + receivers[None]).reshape(group * rows, width)
        edges = layer_norm(dot(silu(hidden).astype(jnp.bfloat16), p_hid[...]))
        for k in range(group):
            one = edges[k * rows : (k + 1) * rows]
            total = one if total is None else total + one
    hidden = dot(mid, u_in[:width]) + dot(total.astype(jnp.bfloat16), u_in[width:])
    hidden = silu(hidden).astype(jnp.bfloat16)
    out = mid.astype(jnp.float32) + layer_norm(dot(hidden, u_hid[...]))
    out_ref[...] = out.astype(jnp.bfloat16)


def shards(
    grid_lat,
    grid_route,
    grid_slot,
    mesh_lat,
    mesh_nbr,
    enc_w1,
    enc_w2,
    grid_w1,
    grid_w2,
    node_w1,
    node_w2,
    proc_w1,
    proc_w2,
    upd_w1,
    upd_w2,
):
    grid_rows, width = grid_lat.shape
    mesh_rows = mesh_lat.shape[0]
    faces = lax.axis_size("face")
    bands, subs = lax.axis_size("band"), lax.axis_size("sub")
    count = bands * subs
    f32, bf16 = jnp.float32, jnp.bfloat16

    def matrix(weight):
        return pltpu.VMEM((weight.shape[0] * count, weight.shape[1]), bf16)

    def cost(rows, depth):
        return pl.CostEstimate(
            flops=2 * rows * depth * width,
            bytes_accessed=2 * (rows + depth) * width,
            transcendentals=rows * width,
        )

    weights = (node_w1, node_w2, grid_w1, grid_w2, proc_w1, proc_w2, upd_w1, upd_w2)
    sizes = [weight.shape[0] for weight in weights]
    groups = lax.axis_size("groups")
    small = pl.CostEstimate(flops=1, bytes_accessed=1, transcendentals=0)
    rows = list(enumerate(sizes))
    halves = [(at, size // groups) for at, size in rows[4:]]
    early, late, part = pack(weights, (rows[:4], rows[4:], halves))
    enc_far = [[shift(one, "band", step) for step in range(1, bands)] for one in (enc_w1, enc_w2)]
    enc_all = [
        own_spread(one) + relay(far, part) for one, far in zip((enc_w1, enc_w2), enc_far)
    ]
    own_enc = enc_all[0][1:subs] + enc_all[1][1:subs]
    part_sent = after(part, *enc_far[0], *enc_far[1], *own_enc)
    part_far = [shift(part_sent, "band", step) for step in range(1, bands)]
    early_near, late_near = own_spread(early), own_spread(late)

    me = lax.axis_index("face")
    routes = grid_route[:, 0]
    steps = distances(faces)
    distance = lax.rem(routes - me + faces, faces) if faces & (faces - 1) else routes ^ me
    targets = (distance * mesh_rows + grid_slot).reshape(1, grid_rows)

    block = (mesh_rows, width)
    sums = pl.pallas_call(
        functools.partial(encode_kernel, count, faces, mesh_rows),
        out_shape=[
            jax.ShapeDtypeStruct(block, bf16 if step else f32) for step in range(faces)
        ],
        in_specs=[VMEM, VMEM] + [VMEM] * (2 * count),
        out_specs=[VMEM] * faces,
        scratch_shapes=[
            matrix(enc_w1),
            matrix(enc_w2),
            pltpu.VMEM((grid_rows, width), bf16),
        ],
        compiler_params=pltpu.CompilerParams(vmem_limit_bytes=16 * MIB),
        cost_estimate=cost(grid_rows, 3 * width),
        name="encode",
    )(targets, grid_lat, *enc_all[0], *enc_all[1])
    early_sent = after(early, sums[0])
    early_far = [shift(early_sent, "band", step) for step in range(1, bands)]
    arrived = [sums[0]] + [to_face(sums[step], step) for step in steps[1:]]
    parts, crossed = [], []
    for one in part_far:
        over = after(one, arrived[steps.index(1)])
        others = [shift(over, "groups", step) for step in range(1, groups)]
        parts += [one] + others
        crossed += others
    early_all = early_near + relay(early_far, *arrived[1:], *crossed)
    grid_out = pl.pallas_call(
        functools.partial(grid_kernel, sizes[:4]),
        out_shape=jax.ShapeDtypeStruct(grid_lat.shape, bf16),
        in_specs=[VMEM] + [VMEM] * len(early_all),
        out_specs=VMEM,
        scratch_shapes=[matrix(grid_w1), matrix(grid_w2)],
        compiler_params=pltpu.CompilerParams(vmem_limit_bytes=16 * MIB),
        cost_estimate=cost(grid_rows, 2 * width),
        name="grid_update",
    )(grid_lat, *early_all)

    half = (mesh_rows // 2, width)
    head, tail = pl.pallas_call(
        functools.partial(node_kernel, sizes[:4], faces),
        out_shape=[jax.ShapeDtypeStruct(half, bf16)] * 2,
        in_specs=[VMEM] * (1 + faces) + [VMEM] * len(early_all),
        out_specs=[VMEM] * 2,
        scratch_shapes=[matrix(node_w1), matrix(node_w2)],
        compiler_params=pltpu.CompilerParams(vmem_limit_bytes=16 * MIB),
        cost_estimate=cost(mesh_rows, 3 * width),
        name="node_update",
    )(mesh_lat, *arrived, *early_all)

    before = shift(tail, "face", 1)
    behind = shift(head, "face", faces - 1)
    late_all = late_near + relay(parts, head)
    mesh_out = pl.pallas_call(
        functools.partial(edge_kernel, sizes[4:]),
        out_shape=jax.ShapeDtypeStruct(mesh_lat.shape, bf16),
        in_specs=[VMEM] * 5 + [VMEM] * len(late_all),
        out_specs=VMEM,
        scratch_shapes=[
            matrix(proc_w1),
            matrix(proc_w2),
            matrix(upd_w1),
            matrix(upd_w2),
        ],
        compiler_params=pltpu.CompilerParams(vmem_limit_bytes=16 * MIB),
        cost_estimate=cost(mesh_rows * mesh_nbr.shape[1], 3 * width),
        name="edge_update",
    )(mesh_nbr, before, head, tail, behind, *late_all)
    return (grid_out, mesh_out)


def solution(mesh):
    rows = ("groups", "face", "band", "sub")
    placed = (
        P(rows, None),
        P(rows, None),
        P(rows),
        P(rows, None),
        P(rows, None),
    ) + (P(("band", "sub"), None),) * 10
    return jax.shard_map(
        shards,
        mesh=mesh,
        in_specs=placed,
        out_specs=(P(rows, None), P(rows, None)),
        check_vma=False,
    )
```

```python
import functools

import jax
import jax.numpy as jnp
from jax import lax
from jax.experimental import pallas as pl
from jax.experimental.pallas import tpu as pltpu
from jax.sharding import PartitionSpec as P

MIB = 1 << 20
VMEM = pl.BlockSpec(memory_space=pltpu.VMEM)


def after(value, *earlier):
    return lax.optimization_barrier((value, *earlier))[0]


def shift(value, axis, step):
    count = lax.axis_size(axis)
    return lax.ppermute(value, axis, [(i, (i + step) % count) for i in range(count)])


def distances(faces):
    if faces & (faces - 1):
        return list(range(faces))
    return [0] + sorted(range(1, faces), key=lambda step: (step == 1, step))


def face_at(faces, step, me):
    return (me + step) % faces if faces & (faces - 1) else me ^ step


def to_face(value, step):
    faces = lax.axis_size("face")
    return lax.ppermute(value, "face", [(i, face_at(faces, step, i)) for i in range(faces)])


def own_spread(pack):
    return [pack] + [shift(pack, "sub", step) for step in range(1, lax.axis_size("sub"))]


def relay(parts, *earlier):
    pieces = []
    for part in parts:
        pieces.extend(own_spread(after(part, *earlier) if earlier else part))
    return pieces


def owner_of(band_step, sub_step):
    bands, subs = lax.axis_size("band"), lax.axis_size("sub")
    return lax.rem(lax.axis_index("band") + bands - band_step, bands) * subs + lax.rem(
        lax.axis_index("sub") + subs - sub_step, subs
    )


def place(pieces, start, rows, whole):
    subs = lax.axis_size("sub")
    for index, piece in enumerate(pieces):
        owner = owner_of(index // subs, index % subs)
        whole[pl.ds(pl.multiple_of(owner * rows, rows), rows)] = piece[start : start + rows]


def unpack(pieces, sizes, wanted):
    for at, whole in wanted.items():
        place(pieces, sum(sizes[:at]), sizes[at], whole)


def pack_kernel(sets, *refs):
    sources, outs = list(refs[: sum(sets)]), refs[sum(sets) :]
    for out, amount in zip(outs, sets):
        start = 0
        for _ in range(amount):
            source = sources.pop(0)
            out[start : start + source.shape[0]] = source[...]
            start += source.shape[0]


def pack(sets):
    width = sets[0][0].shape[1]
    return pl.pallas_call(
        functools.partial(pack_kernel, [len(one) for one in sets]),
        out_shape=[
            jax.ShapeDtypeStruct((sum(weight.shape[0] for weight in one), width), jnp.bfloat16)
            for one in sets
        ],
        in_specs=[VMEM] * sum(len(one) for one in sets),
        out_specs=[VMEM] * len(sets),
        name="pack",
    )(*(weight for one in sets for weight in one))


def silu(values):
    half = 0.5 * values
    return half + half * jnp.tanh(half)


def layer_norm(values):
    average = jnp.mean(values, axis=-1, keepdims=True)
    centred = values - average
    spread_of = jnp.mean(centred * centred, axis=-1, keepdims=True)
    return centred * lax.rsqrt(spread_of + 1e-05)


def dot(a, b):
    return jnp.dot(a, b, preferred_element_type=jnp.float32)


def encode_kernel(count, faces, mesh_rows, target_ref, lat_ref, *refs):
    in_pieces, hid_pieces = refs[:count], refs[count : 2 * count]
    outs = refs[2 * count : 2 * count + faces]
    w_in, w_hid, messages = refs[2 * count + faces :]
    rows = w_in.shape[0] // count
    place(in_pieces, 0, rows, w_in)
    place(hid_pieces, 0, rows, w_hid)
    block = 256
    for start in range(0, lat_ref.shape[0], block):
        here = pl.ds(start, block)
        hidden = silu(dot(lat_ref[here], w_in[...])).astype(jnp.bfloat16)
        messages[here] = layer_norm(dot(hidden, w_hid[...])).astype(jnp.bfloat16)
    group = min(faces, 4)
    for at in range(0, faces, group):
        slots = lax.broadcasted_iota(jnp.int32, (group * mesh_rows, lat_ref.shape[0]), 0)
        chosen = jnp.where(slots + at * mesh_rows == target_ref[...], 1.0, 0.0)
        chosen = chosen.astype(jnp.bfloat16)
        sums = dot(chosen, messages[...])
        for face in range(group):
            out = outs[at + face]
            out[...] = sums[face * mesh_rows : (face + 1) * mesh_rows].astype(out.dtype)


def grid_kernel(sizes, lat_ref, *refs):
    pieces, (out_ref, w_in, w_hid) = refs[:-3], refs[-3:]
    unpack(pieces, sizes, {2: w_in, 3: w_hid})
    block = 256
    for start in range(0, lat_ref.shape[0], block):
        here = pl.ds(start, block)
        lat = lat_ref[here]
        hidden = silu(dot(lat, w_in[...])).astype(jnp.bfloat16)
        out = lat.astype(jnp.float32) + layer_norm(dot(hidden, w_hid[...]))
        out_ref[here] = out.astype(jnp.bfloat16)


def node_kernel(sizes, faces, lat_ref, *refs):
    sums, pieces = refs[:faces], refs[faces:-4]
    head_ref, tail_ref, w_in, w_hid = refs[-4:]
    width = lat_ref.shape[1]
    unpack(pieces, sizes, {0: w_in, 1: w_hid})
    collected = sums[0][...]
    for one in sums[1:]:
        collected = collected + one[...].astype(jnp.float32)
    lat = lat_ref[...]
    hidden = dot(lat, w_in[:width]) + dot(collected.astype(jnp.bfloat16), w_in[width:])
    hidden = silu(hidden).astype(jnp.bfloat16)
    mid = lat.astype(jnp.float32) + layer_norm(dot(hidden, w_hid[...]))
    mid = mid.astype(jnp.bfloat16)
    half = mid.shape[0] // 2
    head_ref[...] = mid[:half]
    tail_ref[...] = mid[half:]


def share(inputs_ref, piece, index, rows):
    subs = lax.axis_size("sub")
    start = pl.multiple_of(owner_of(index // subs, index % subs) * rows, rows)
    return dot(inputs_ref[:, pl.ds(start, rows)], piece[:rows])


def prepare_kernel(here, depth, nbr_ref, before_ref, head_ref, tail_ref, after_ref, *refs):
    pieces, (inputs_ref, hidden_ref) = refs[:-2], refs[-2:]
    rows, fanin = nbr_ref.shape
    width = head_ref.shape[1]
    mid = jnp.concatenate([head_ref[...], tail_ref[...]], axis=0)
    extended = jnp.concatenate([before_ref[...], mid, after_ref[...]], axis=0)
    spots = lax.broadcasted_iota(jnp.int32, (rows, extended.shape[0]), 1)
    nbr = nbr_ref[...]
    for k in range(fanin):
        chosen = jnp.where(spots == nbr[:, k : k + 1], 1.0, 0.0).astype(jnp.bfloat16)
        edges = pl.ds(k * rows, rows)
        inputs_ref[edges, :width] = dot(chosen, extended).astype(jnp.bfloat16)
        inputs_ref[edges, width:] = mid
    hidden = None
    for index, piece in zip(here, pieces):
        one = share(inputs_ref, piece, index, depth)
        hidden = one if hidden is None else hidden + one
    hidden_ref[...] = hidden


def edge_kernel(sizes, missing, head_ref, tail_ref, inputs_ref, hidden_ref, *refs):
    pieces, (out_ref, p_hid, u_in, u_hid) = refs[:-4], refs[-4:]
    unpack(pieces, sizes, {1: p_hid, 2: u_in, 3: u_hid})
    width = head_ref.shape[1]
    mid = jnp.concatenate([head_ref[...], tail_ref[...]], axis=0)
    rows = mid.shape[0]
    hidden = hidden_ref[...]
    for index in missing:
        hidden = hidden + share(inputs_ref, pieces[index], index, sizes[0])
    edges = layer_norm(dot(silu(hidden).astype(jnp.bfloat16), p_hid[...]))
    total = edges[:rows]
    for start in range(rows, edges.shape[0], rows):
        total = total + edges[start : start + rows]
    hidden = dot(mid, u_in[:width]) + dot(total.astype(jnp.bfloat16), u_in[width:])
    hidden = silu(hidden).astype(jnp.bfloat16)
    out = mid.astype(jnp.float32) + layer_norm(dot(hidden, u_hid[...]))
    out_ref[...] = out.astype(jnp.bfloat16)


def shards(
    grid_lat,
    grid_route,
    grid_slot,
    mesh_lat,
    mesh_nbr,
    enc_w1,
    enc_w2,
    grid_w1,
    grid_w2,
    node_w1,
    node_w2,
    proc_w1,
    proc_w2,
    upd_w1,
    upd_w2,
):
    grid_rows, width = grid_lat.shape
    mesh_rows = mesh_lat.shape[0]
    faces = lax.axis_size("face")
    bands, subs = lax.axis_size("band"), lax.axis_size("sub")
    count = bands * subs
    f32, bf16 = jnp.float32, jnp.bfloat16

    def matrix(weight):
        return pltpu.VMEM((weight.shape[0] * count, weight.shape[1]), bf16)

    def cost(rows, depth):
        return pl.CostEstimate(
            flops=2 * rows * depth * width,
            bytes_accessed=2 * (rows + depth) * width,
            transcendentals=rows * width,
        )

    sets = ((node_w1, node_w2, grid_w1, grid_w2), (proc_w1, proc_w2, upd_w1, upd_w2))
    sizes = [[weight.shape[0] for weight in one] for one in sets]
    enc_far = [[shift(one, "band", step) for step in range(1, bands)] for one in (enc_w1, enc_w2)]
    enc_all = [
        own_spread(one) + relay(far) for one, far in zip((enc_w1, enc_w2), enc_far)
    ]
    early, late = pack(sets)
    early_sent = after(early, *enc_far[0], *enc_far[1], *enc_all[0][1:subs], *enc_all[1][1:subs])
    early_far = [shift(early_sent, "band", step) for step in range(1, bands)]
    early_near, late_near = own_spread(early), own_spread(late)

    me = lax.axis_index("face")
    routes = grid_route[:, 0]
    steps = distances(faces)
    distance = lax.rem(routes - me + faces, faces) if faces & (faces - 1) else routes ^ me
    targets = (distance * mesh_rows + grid_slot).reshape(1, grid_rows)

    block = (mesh_rows, width)
    sums = pl.pallas_call(
        functools.partial(encode_kernel, count, faces, mesh_rows),
        out_shape=[
            jax.ShapeDtypeStruct(block, bf16 if step else f32) for step in range(faces)
        ],
        in_specs=[VMEM, VMEM] + [VMEM] * (2 * count),
        out_specs=[VMEM] * faces,
        scratch_shapes=[
            matrix(enc_w1),
            matrix(enc_w2),
            pltpu.VMEM((grid_rows, width), bf16),
        ],
        compiler_params=pltpu.CompilerParams(vmem_limit_bytes=16 * MIB),
        cost_estimate=cost(grid_rows, 3 * width),
        name="encode",
    )(targets, grid_lat, *enc_all[0], *enc_all[1])
    late_sent = after(late, sums[0])
    late_far = [shift(late_sent, "band", step) for step in range(1, bands)]
    arrived = [sums[0]] + [to_face(sums[step], step) for step in steps[1:]]

    early_all = early_near + relay(early_far, *arrived[1:])
    grid_out = pl.pallas_call(
        functools.partial(grid_kernel, sizes[0]),
        out_shape=jax.ShapeDtypeStruct(grid_lat.shape, bf16),
        in_specs=[VMEM] + [VMEM] * len(early_all),
        out_specs=VMEM,
        scratch_shapes=[matrix(grid_w1), matrix(grid_w2)],
        compiler_params=pltpu.CompilerParams(vmem_limit_bytes=16 * MIB),
        cost_estimate=cost(grid_rows, 2 * width),
        name="grid_update",
    )(grid_lat, *early_all)

    half = (mesh_rows // 2, width)
    head, tail = pl.pallas_call(
        functools.partial(node_kernel, sizes[0], faces),
        out_shape=[jax.ShapeDtypeStruct(half, bf16)] * 2,
        in_specs=[VMEM] * (1 + faces) + [VMEM] * len(early_all),
        out_specs=[VMEM] * 2,
        scratch_shapes=[matrix(node_w1), matrix(node_w2)],
        compiler_params=pltpu.CompilerParams(vmem_limit_bytes=16 * MIB),
        cost_estimate=cost(mesh_rows, 3 * width),
        name="node_update",
    )(mesh_lat, *arrived, *early_all)

    before = shift(tail, "face", 1)
    behind = shift(head, "face", faces - 1)
    late_all = late_near + relay(late_far, before, behind, grid_out)
    here = [at for at in range(count) if at < subs or at % subs == 0]
    missing = [at for at in range(count) if at not in here]
    edges = mesh_rows * mesh_nbr.shape[1]
    inputs, hidden = pl.pallas_call(
        functools.partial(prepare_kernel, here, proc_w1.shape[0]),
        out_shape=[
            jax.ShapeDtypeStruct((edges, 2 * width), bf16),
            jax.ShapeDtypeStruct((edges, width), jnp.float32),
        ],
        in_specs=[VMEM] * (5 + len(here)),
        out_specs=[VMEM] * 2,
        compiler_params=pltpu.CompilerParams(vmem_limit_bytes=16 * MIB),
        cost_estimate=cost(edges, 2 * width),
        name="prepare",
    )(mesh_nbr, before, head, tail, behind, *(late_all[at] for at in here))
    mesh_out = pl.pallas_call(
        functools.partial(edge_kernel, sizes[1], missing),
        out_shape=jax.ShapeDtypeStruct(mesh_lat.shape, bf16),
        in_specs=[VMEM] * (4 + count),
        out_specs=VMEM,
        scratch_shapes=[matrix(proc_w2), matrix(upd_w1), matrix(upd_w2)],
        compiler_params=pltpu.CompilerParams(vmem_limit_bytes=16 * MIB),
        cost_estimate=cost(edges, 2 * width),
        name="edge_update",
    )(head, tail, inputs, hidden, *late_all)
    return (grid_out, mesh_out)


def solution(mesh):
    rows = ("groups", "face", "band", "sub")
    placed = (
        P(rows, None),
        P(rows, None),
        P(rows),
        P(rows, None),
        P(rows, None),
    ) + (P(("band", "sub"), None),) * 10
    return jax.shard_map(
        shards,
        mesh=mesh,
        in_specs=placed,
        out_specs=(P(rows, None), P(rows, None)),
        check_vma=False,
    )
```

```python
import functools

import jax
import jax.numpy as jnp
from jax import lax
from jax.experimental import pallas as pl
from jax.experimental.pallas import tpu as pltpu
from jax.sharding import PartitionSpec as P

MIB = 1 << 20
VMEM = pl.BlockSpec(memory_space=pltpu.VMEM)
HBM = pl.BlockSpec(memory_space=pltpu.HBM)


def after(value, *earlier):
    return lax.optimization_barrier((value, *earlier))[0]


def shift(value, axis, step):
    count = lax.axis_size(axis)
    return lax.ppermute(value, axis, [(i, (i + step) % count) for i in range(count)])


def distances(faces):
    if faces & (faces - 1):
        return list(range(faces))
    return [0] + sorted(range(1, faces), key=lambda step: (step == 1, step))


def face_at(faces, step, me):
    return (me + step) % faces if faces & (faces - 1) else me ^ step


def to_face(value, step):
    faces = lax.axis_size("face")
    return lax.ppermute(value, "face", [(i, face_at(faces, step, i)) for i in range(faces)])


def own_spread(pack):
    return [pack] + [shift(pack, "sub", step) for step in range(1, lax.axis_size("sub"))]


def relay(parts, *earlier):
    pieces = []
    for part in parts:
        pieces.extend(own_spread(after(part, *earlier) if earlier else part))
    return pieces


def owner_of(band_step, sub_step):
    bands, subs = lax.axis_size("band"), lax.axis_size("sub")
    return lax.rem(lax.axis_index("band") + bands - band_step, bands) * subs + lax.rem(
        lax.axis_index("sub") + subs - sub_step, subs
    )


def place(pieces, start, rows, whole):
    subs = lax.axis_size("sub")
    for index, piece in enumerate(pieces):
        owner = owner_of(index // subs, index % subs)
        whole[pl.ds(pl.multiple_of(owner * rows, rows), rows)] = piece[start : start + rows]


def unpack(pieces, sizes, wanted):
    for at, whole in wanted.items():
        place(pieces, sum(sizes[:at]), sizes[at], whole)


def pack_kernel(sets, *refs):
    sources, outs = list(refs[: sum(sets)]), refs[sum(sets) :]
    for out, amount in zip(outs, sets):
        start = 0
        for _ in range(amount):
            source = sources.pop(0)
            out[start : start + source.shape[0]] = source[...]
            start += source.shape[0]


def pack(sets):
    width = sets[0][0].shape[1]
    return pl.pallas_call(
        functools.partial(pack_kernel, [len(one) for one in sets]),
        out_shape=[
            jax.ShapeDtypeStruct((sum(weight.shape[0] for weight in one), width), jnp.bfloat16)
            for one in sets
        ],
        in_specs=[VMEM] * sum(len(one) for one in sets),
        out_specs=[VMEM] * len(sets),
        name="pack",
    )(*(weight for one in sets for weight in one))


def silu(values):
    half = 0.5 * values
    return half + half * jnp.tanh(half)


def layer_norm(values):
    average = jnp.mean(values, axis=-1, keepdims=True)
    centred = values - average
    spread_of = jnp.mean(centred * centred, axis=-1, keepdims=True)
    return centred * lax.rsqrt(spread_of + 1e-05)


def dot(a, b):
    return jnp.dot(a, b, preferred_element_type=jnp.float32)


def encode_kernel(count, faces, mesh_rows, route_ref, slot_ref, lat_hbm, *refs):
    in_pieces, hid_pieces = refs[:count], refs[count : 2 * count]
    outs = refs[2 * count : 2 * count + faces]
    w_in, w_hid, messages, lat_ref, sems = refs[2 * count + faces :]
    rows = w_in.shape[0] // count
    block = 256
    starts = range(0, lat_ref.shape[0], block)
    copies = [
        pltpu.make_async_copy(lat_hbm.at[pl.ds(at, block)], lat_ref.at[pl.ds(at, block)], sems.at[2 + at // block])
        for at in starts
    ]
    own = pl.ds(pl.multiple_of(owner_of(0, 0) * rows, rows), rows)
    own_copies = [
        pltpu.make_async_copy(pieces[0], whole.at[own], sems.at[at])
        for at, (pieces, whole) in enumerate([(in_pieces, w_in), (hid_pieces, w_hid)])
    ]
    for copy in own_copies + copies:
        copy.start()
    subs = lax.axis_size("sub")
    for pieces, whole in ((in_pieces, w_in), (hid_pieces, w_hid)):
        for index in range(1, count):
            owner = owner_of(index // subs, index % subs)
            whole[pl.ds(pl.multiple_of(owner * rows, rows), rows)] = pieces[index][...]
    me = lax.axis_index("face")
    routes = route_ref[...]
    distance = lax.rem(routes - me + faces, faces) if faces & (faces - 1) else routes ^ me
    targets = distance * mesh_rows + slot_ref[...]
    for copy in own_copies:
        copy.wait()
    for copy, start in zip(copies, starts):
        here = pl.ds(start, block)
        copy.wait()
        hidden = silu(dot(lat_ref[here], w_in[...])).astype(jnp.bfloat16)
        messages[here] = layer_norm(dot(hidden, w_hid[...])).astype(jnp.bfloat16)
    group = min(faces, 4)
    for at in range(0, faces, group):
        slots = lax.broadcasted_iota(jnp.int32, (group * mesh_rows, lat_ref.shape[0]), 0)
        chosen = jnp.where(slots + at * mesh_rows == targets, 1.0, 0.0)
        chosen = chosen.astype(jnp.bfloat16)
        sums = dot(chosen, messages[...])
        for face in range(group):
            out = outs[at + face]
            out[...] = sums[face * mesh_rows : (face + 1) * mesh_rows].astype(out.dtype)


def grid_kernel(sizes, lat_ref, *refs):
    pieces, (out_ref, w_in, w_hid) = refs[:-3], refs[-3:]
    unpack(pieces, sizes, {2: w_in, 3: w_hid})
    block = 256
    for start in range(0, lat_ref.shape[0], block):
        here = pl.ds(start, block)
        lat = lat_ref[here]
        hidden = silu(dot(lat, w_in[...])).astype(jnp.bfloat16)
        out = lat.astype(jnp.float32) + layer_norm(dot(hidden, w_hid[...]))
        out_ref[here] = out.astype(jnp.bfloat16)


def node_kernel(sizes, faces, lat_ref, *refs):
    sums, pieces = refs[:faces], refs[faces:-4]
    head_ref, tail_ref, w_in, w_hid = refs[-4:]
    width = lat_ref.shape[1]
    unpack(pieces, sizes, {0: w_in, 1: w_hid})
    collected = sums[0][...]
    for one in sums[1:]:
        collected = collected + one[...].astype(jnp.float32)
    lat = lat_ref[...]
    hidden = dot(lat, w_in[:width]) + dot(collected.astype(jnp.bfloat16), w_in[width:])
    hidden = silu(hidden).astype(jnp.bfloat16)
    mid = lat.astype(jnp.float32) + layer_norm(dot(hidden, w_hid[...]))
    mid = mid.astype(jnp.bfloat16)
    half = mid.shape[0] // 2
    head_ref[...] = mid[:half]
    tail_ref[...] = mid[half:]


def share(inputs_ref, piece, index, rows):
    subs = lax.axis_size("sub")
    start = pl.multiple_of(owner_of(index // subs, index % subs) * rows, rows)
    return dot(inputs_ref[:, pl.ds(start, rows)], piece[:rows])


def prepare_kernel(here, depth, nbr_ref, before_ref, head_ref, tail_ref, after_ref, *refs):
    pieces, (inputs_ref, hidden_ref) = refs[:-2], refs[-2:]
    rows, fanin = nbr_ref.shape
    width = head_ref.shape[1]
    mid = jnp.concatenate([head_ref[...], tail_ref[...]], axis=0)
    extended = jnp.concatenate([before_ref[...], mid, after_ref[...]], axis=0)
    spots = lax.broadcasted_iota(jnp.int32, (rows, extended.shape[0]), 1)
    nbr = nbr_ref[...]
    for k in range(fanin):
        chosen = jnp.where(spots == nbr[:, k : k + 1], 1.0, 0.0).astype(jnp.bfloat16)
        edges = pl.ds(k * rows, rows)
        inputs_ref[edges, :width] = dot(chosen, extended).astype(jnp.bfloat16)
        inputs_ref[edges, width:] = mid
    hidden = None
    for index, piece in zip(here, pieces):
        one = share(inputs_ref, piece, index, depth)
        hidden = one if hidden is None else hidden + one
    hidden_ref[...] = hidden


def edge_kernel(sizes, missing, head_ref, tail_ref, inputs_ref, hidden_ref, *refs):
    pieces, (out_ref, p_hid, u_in, u_hid) = refs[:-4], refs[-4:]
    unpack(pieces, sizes, {1: p_hid, 2: u_in, 3: u_hid})
    width = head_ref.shape[1]
    mid = jnp.concatenate([head_ref[...], tail_ref[...]], axis=0)
    rows = mid.shape[0]
    hidden = hidden_ref[...]
    for index in missing:
        hidden = hidden + share(inputs_ref, pieces[index], index, sizes[0])
    edges = layer_norm(dot(silu(hidden).astype(jnp.bfloat16), p_hid[...]))
    total = edges[:rows]
    for start in range(rows, edges.shape[0], rows):
        total = total + edges[start : start + rows]
    hidden = dot(mid, u_in[:width]) + dot(total.astype(jnp.bfloat16), u_in[width:])
    hidden = silu(hidden).astype(jnp.bfloat16)
    out = mid.astype(jnp.float32) + layer_norm(dot(hidden, u_hid[...]))
    out_ref[...] = out.astype(jnp.bfloat16)


def shards(
    grid_lat,
    grid_route,
    grid_slot,
    mesh_lat,
    mesh_nbr,
    enc_w1,
    enc_w2,
    grid_w1,
    grid_w2,
    node_w1,
    node_w2,
    proc_w1,
    proc_w2,
    upd_w1,
    upd_w2,
):
    grid_rows, width = grid_lat.shape
    mesh_rows = mesh_lat.shape[0]
    faces = lax.axis_size("face")
    bands, subs = lax.axis_size("band"), lax.axis_size("sub")
    count = bands * subs
    f32, bf16 = jnp.float32, jnp.bfloat16

    def matrix(weight):
        return pltpu.VMEM((weight.shape[0] * count, weight.shape[1]), bf16)

    def cost(rows, depth):
        return pl.CostEstimate(
            flops=2 * rows * depth * width,
            bytes_accessed=2 * (rows + depth) * width,
            transcendentals=rows * width,
        )

    sets = ((node_w1, node_w2, grid_w1, grid_w2), (proc_w1, proc_w2, upd_w1, upd_w2))
    sizes = [[weight.shape[0] for weight in one] for one in sets]
    enc_far = [[shift(one, "band", step) for step in range(1, bands)] for one in (enc_w1, enc_w2)]
    enc_all = [
        own_spread(one) + relay(far) for one, far in zip((enc_w1, enc_w2), enc_far)
    ]
    early, late = pack(sets)
    early_sent = after(early, *enc_far[0], *enc_far[1], *enc_all[0][1:subs], *enc_all[1][1:subs])
    early_far = [shift(early_sent, "band", step) for step in range(1, bands)]
    early_near, late_near = own_spread(early), own_spread(late)

    steps = distances(faces)
    block = (mesh_rows, width)
    sums = pl.pallas_call(
        functools.partial(encode_kernel, count, faces, mesh_rows),
        out_shape=[
            jax.ShapeDtypeStruct(block, bf16 if step else f32) for step in range(faces)
        ],
        in_specs=[VMEM] * 2 + ([HBM] + [HBM] + [VMEM] * (count - 1) + [HBM] + [VMEM] * (count - 1)),
        out_specs=[VMEM] * faces,
        scratch_shapes=[
            matrix(enc_w1),
            matrix(enc_w2),
            pltpu.VMEM((grid_rows, width), bf16),
            pltpu.VMEM((grid_rows, width), bf16),
            pltpu.SemaphoreType.DMA((2 + grid_rows // 256,)),
        ],
        compiler_params=pltpu.CompilerParams(vmem_limit_bytes=16 * MIB),
        cost_estimate=cost(grid_rows, 3 * width),
        name="encode",
    )(grid_route.reshape(1, grid_rows), grid_slot.reshape(1, grid_rows), grid_lat, *enc_all[0], *enc_all[1])
    late_sent = after(late, sums[0])
    late_far = [shift(late_sent, "band", step) for step in range(1, bands)]
    arrived = [sums[0]] + [to_face(sums[step], step) for step in steps[1:]]

    early_all = early_near + relay(early_far, *arrived[1:])
    grid_out = pl.pallas_call(
        functools.partial(grid_kernel, sizes[0]),
        out_shape=jax.ShapeDtypeStruct(grid_lat.shape, bf16),
        in_specs=[VMEM] + [VMEM] * len(early_all),
        out_specs=VMEM,
        scratch_shapes=[matrix(grid_w1), matrix(grid_w2)],
        compiler_params=pltpu.CompilerParams(vmem_limit_bytes=16 * MIB),
        cost_estimate=cost(grid_rows, 2 * width),
        name="grid_update",
    )(grid_lat, *early_all)

    half = (mesh_rows // 2, width)
    head, tail = pl.pallas_call(
        functools.partial(node_kernel, sizes[0], faces),
        out_shape=[jax.ShapeDtypeStruct(half, bf16)] * 2,
        in_specs=[VMEM] * (1 + faces) + [VMEM] * len(early_all),
        out_specs=[VMEM] * 2,
        scratch_shapes=[matrix(node_w1), matrix(node_w2)],
        compiler_params=pltpu.CompilerParams(vmem_limit_bytes=16 * MIB),
        cost_estimate=cost(mesh_rows, 3 * width),
        name="node_update",
    )(mesh_lat, *arrived, *early_all)

    before = shift(tail, "face", 1)
    behind = shift(head, "face", faces - 1)
    late_all = late_near + relay(late_far, before, behind, grid_out)
    here = [at for at in range(count) if at < subs or at % subs == 0]
    missing = [at for at in range(count) if at not in here]
    edges = mesh_rows * mesh_nbr.shape[1]
    inputs, hidden = pl.pallas_call(
        functools.partial(prepare_kernel, here, proc_w1.shape[0]),
        out_shape=[
            jax.ShapeDtypeStruct((edges, 2 * width), bf16),
            jax.ShapeDtypeStruct((edges, width), jnp.float32),
        ],
        in_specs=[VMEM] * (5 + len(here)),
        out_specs=[VMEM] * 2,
        compiler_params=pltpu.CompilerParams(vmem_limit_bytes=16 * MIB),
        cost_estimate=cost(edges, 2 * width),
        name="prepare",
    )(mesh_nbr, before, head, tail, behind, *(late_all[at] for at in here))
    mesh_out = pl.pallas_call(
        functools.partial(edge_kernel, sizes[1], missing),
        out_shape=jax.ShapeDtypeStruct(mesh_lat.shape, bf16),
        in_specs=[VMEM] * (4 + count),
        out_specs=VMEM,
        scratch_shapes=[matrix(proc_w2), matrix(upd_w1), matrix(upd_w2)],
        compiler_params=pltpu.CompilerParams(vmem_limit_bytes=16 * MIB),
        cost_estimate=cost(edges, 2 * width),
        name="edge_update",
    )(head, tail, inputs, hidden, *late_all)
    return (grid_out, mesh_out)


def solution(mesh):
    rows = ("groups", "face", "band", "sub")
    placed = (
        P(rows, None),
        P(rows, None),
        P(rows),
        P(rows, None),
        P(rows, None),
    ) + (P(("band", "sub"), None),) * 10
    return jax.shard_map(
        shards,
        mesh=mesh,
        in_specs=placed,
        out_specs=(P(rows, None), P(rows, None)),
        check_vma=False,
    )
```
